768 devices in a mesh: latent: 8 (over y_lo, core), dp: 96 (over z, y_hi, x).
Axes of the slice: x: 4, y: 8 (y_hi: 2, y_lo: 4; y = y_hi * 4 + y_lo), z: 12, core: 2. Of those that a mesh axis runs over, the one named last changes fastest.
Arguments:
- activations: bfloat16 [12288, 8192], P('dp'), may hold values from -20 to 20
- weight: float32 [768, 8192], P(('latent', 'dp')), may hold values from -2 to 2
- weight_mean: float32 [768, 8192], P(('latent', 'dp')), may hold values from -0.02 to 0.02
- weight_square: float32 [768, 8192], P(('latent', 'dp')), may hold values from 3e-05 to 0.003
- code_bias: float32 [768], P('latent'), may hold values from -3 to 3
- bias_mean: float32 [768], P('latent'), may hold values from -2 to 2
- bias_square: float32 [768], P('latent'), may hold values from 0.1 to 4
Outputs:
- after_weight: float32 [768, 8192], P(('latent', 'dp'))
- after_mean: float32 [768, 8192], P(('latent', 'dp'))
- after_square: float32 [768, 8192], P(('latent', 'dp'))
- after_bias: float32 [768], P('latent')
- after_biasmean: float32 [768], P('latent')
- after_biassquare: float32 [768], P('latent')
- total_loss: float32 [], replicated
The draws below stay inside these ranges and needn't reach their ends.
All inputs are finite; a program needn't handle non-finite values.
Results may differ from the reference program's by a relative error of at most 0.023.
Values may be sent and summed in bfloat16 or wider, within the bound.
A program may use at most 32 MiB of HBM per device.

```python
import math
import jax
import jax.numpy as jnp
from jax import lax

D = 8192
BLOCK = 96
LATENTS = 768
TOKENS = 12288
N_LATENT = 8


def draw_activations(key, part):
    key = jax.random.fold_in(key, 11)
    first, second = jax.random.split(key, 2)
    places = jnp.arange(TOKENS, dtype=jnp.float32)
    rising = 0.5 + places / TOKENS
    columns = jnp.arange(D, dtype=jnp.float32) / D
    spread = jnp.exp(jax.random.uniform(second, (TOKENS, 1), jnp.float32, -1.15, 1.15))
    base = jax.random.truncated_normal(first, -4.0, 4.0, (TOKENS, D), jnp.float32)
    slope = 0.25 + 0.75 * columns
    return (base * spread * rising[:, None] * slope[None, :]).astype(jnp.bfloat16)


def draw_weight(key, part):
    key = jax.random.fold_in(key, 23)
    first, second = jax.random.split(key, 2)
    places = jnp.arange(LATENTS, dtype=jnp.float32)
    rising = 0.6 + 1.2 * places / LATENTS
    spread = jnp.exp(jax.random.uniform(second, (LATENTS, 1), jnp.float32, -0.6, 0.6))
    base = jax.random.truncated_normal(first, -4.0, 4.0, (LATENTS, D), jnp.float32)
    return base * spread * rising[:, None] * D ** (-0.5)


def shard_levels(key, extent, pieces, smallest, largest):
    gain, own = 1.0, jax.random.fold_in(key, 6)
    for axis_at, parts in pieces:
        heights = jnp.exp(jax.random.uniform(jax.random.fold_in(own, axis_at), (parts,), jnp.float32, smallest / len(pieces), largest / len(pieces)))
        gain = gain * jnp.repeat(heights, extent[axis_at] // parts).reshape([-1 if axis == axis_at else 1 for axis in range(len(extent))])
    return gain


def centred(stream_key, shape, width, bound, cuts=(), kind=jnp.bfloat16):
    array = width * jax.random.normal(stream_key, shape, jnp.float32)
    if cuts:
        array = array * shard_levels(stream_key, shape, cuts, -0.22, 0.18)
    return jnp.clip(array, -bound, bound).astype(kind)


def setup_inputs(seed: int = 0) -> dict:
    key_of = jax.random.split(jax.random.key(seed), 8)
    activations = draw_activations(jax.random.fold_in(key_of[7], 71), 0)
    weight = draw_weight(jax.random.fold_in(key_of[7], 71), 0)
    weight_mean = centred(key_of[2], (LATENTS, D), 0.003, 0.02, ((0, 768),), jnp.float32)
    weight_square = jnp.clip(jnp.exp(math.log(0.003) - 4.6051702 * jax.random.uniform(key_of[3], (LATENTS, D), jnp.float32) ** shard_levels(key_of[3], (LATENTS, D), ((0, 768),), -0.2, 0.2)), 2.9999999242136255e-05, 0.003)
    code_bias = centred(key_of[4], (LATENTS,), 0.5, 3.0, ((0, 8),), jnp.float32)
    bias_mean = centred(key_of[5], (LATENTS,), 0.3, 2.0, ((0, 8),), jnp.float32)
    bias_square = jnp.clip(jnp.exp(math.log(4.0) - 3.6888794 * jax.random.uniform(key_of[6], (LATENTS,), jnp.float32) ** shard_levels(key_of[6], (LATENTS,), ((0, 8),), -0.2, 0.2)), 0.1, 4.0)
    return dict(activations=activations, weight=weight, weight_mean=weight_mean, weight_square=weight_square, code_bias=code_bias, bias_mean=bias_mean, bias_square=bias_square)


sparsity = 2.0
first_decay = 0.9
second_decay = 0.999
learn_rate = 0.002
adam_floor = 1e-08
first_fix = 0.9999734386011124
second_fix = 0.09520785288629108

def adam_step(value, mean, square, grad):
    mean_new = first_decay * mean + (1.0 - first_decay) * grad
    square_new = second_decay * square + (1.0 - second_decay) * grad * grad
    value_new = value - learn_rate * (mean_new / first_fix) / (jnp.sqrt(square_new / second_fix) + adam_floor)
    return (value_new, mean_new, square_new)

def reference(activations, weight, weight_mean, weight_square, code_bias, bias_mean, bias_square):
    rows = weight.astype(jnp.bfloat16)
    rows_wide = rows.astype(jnp.float32)
    pre = jnp.dot(activations, rows.T, preferred_element_type=jnp.float32) + code_bias[None, :]
    codes = jnp.maximum(pre, 0.0)
    codes_low = codes.astype(jnp.bfloat16)
    recon = jnp.zeros(activations.shape, jnp.float32)
    for slab in range(N_LATENT):
        lower = slab * BLOCK
        upper = lower + BLOCK
        partial_value = jnp.dot(codes_low[:, lower:upper], rows[lower:upper], preferred_element_type=jnp.float32)
        partial_value = lax.optimization_barrier(partial_value.astype(jnp.bfloat16))
        recon = recon + partial_value.astype(jnp.float32)
    error = recon - activations.astype(jnp.float32)
    norms = jnp.sqrt(lax.optimization_barrier(jnp.sum(rows_wide * rows_wide, axis=1)) + 1e-06)
    squared = jnp.sum(error * error)
    penalty = jnp.sum(codes * norms[None, :])
    total_loss = (squared + sparsity * penalty) / TOKENS
    delta = (2.0 / TOKENS * error).astype(jnp.bfloat16)
    dcode = jnp.dot(delta, rows.T, preferred_element_type=jnp.float32) + sparsity / TOKENS * norms[None, :]
    dpre = jnp.where(pre > 0, dcode, 0.0)
    dpre_low = dpre.astype(jnp.bfloat16)
    counts = lax.optimization_barrier(jnp.sum(codes, axis=0))
    grad = jnp.dot(codes_low.T, delta, preferred_element_type=jnp.float32)
    grad = grad + jnp.dot(dpre_low.T, activations, preferred_element_type=jnp.float32)
    grad = grad + (sparsity / TOKENS * counts / norms)[:, None] * rows_wide
    bias_grad = lax.optimization_barrier(jnp.sum(dpre, axis=0))
    after_weight, after_mean, after_square = adam_step(weight, weight_mean, weight_square, grad)
    after_bias, after_biasmean, after_biassquare = adam_step(code_bias, bias_mean, bias_square, bias_grad)
    return (after_weight, after_mean, after_square, after_bias, after_biasmean, after_biassquare, total_loss)
```

```python
import functools

import jax
import jax.numpy as jnp
from jax import lax
from jax.experimental import pallas as pl
from jax.experimental.pallas import tpu as pltpu
from jax.sharding import PartitionSpec as P

sparsity = 2.0
first_decay = 0.9
second_decay = 0.999
learn_rate = 0.002
adam_floor = 1e-08
first_fix = 0.9999734386011124
second_fix = 0.09520785288629108

TOKENS = 12288
MESH = pl.DeviceIdType.MESH
bf16 = jnp.bfloat16
f32 = jnp.float32


def adam_step(value, mean, square, grad):
    mean_new = first_decay * mean + (1.0 - first_decay) * grad
    square_new = second_decay * square + (1.0 - second_decay) * grad * grad
    value_new = value - learn_rate * (mean_new / first_fix) / (
        jnp.sqrt(square_new / second_fix) + adam_floor
    )
    return (value_new, mean_new, square_new)


def split3(v):
    hi = v.astype(bf16)
    rest = v - hi.astype(f32)
    mid = rest.astype(bf16)
    low = (rest - mid.astype(f32)).astype(bf16)
    return hi, mid, low


def nt(a, b):
    return lax.dot_general(a, b, (((1,), (1,)), ((), ())), preferred_element_type=f32)


def nn(a, b):
    return jnp.dot(a, b, preferred_element_type=f32)


def fold(v):
    total = v[:, 0:128]
    for i in range(1, v.shape[1] // 128):
        total = total + v[:, i * 128 : (i + 1) * 128]
    return total


def kernel(
    act, w_ref, bias_ref, grad_ref, small_ref,
    rbuf, W, DA, LT, pq, pr, C, rown, rs, rr, dq, dr, E, gs, gr, hs, hr, hown, fs, fr,
    vx, vy, vz, vc, hot,
    a_sem, own_sem,
    p0_s, p0_r, agx_s, agx_r, right_s, right_r, left_s, left_r,
    pre_s, pre_r, code_s, code_r, core_s, core_r, dc_s, dc_r, dp_s, dp_r,
    gx_s, gx_r, gz_s, gz_r, fin_s, fin_r, vx_s, vx_r, vy_s, vy_r, vz_s, vz_r, vc_s, vc_r,
):
    l = lax.axis_index("latent")
    g = lax.axis_index("dp")
    q, c = lax.div(l, 2), lax.rem(l, 2)
    x, yh, z = lax.rem(g, 4), lax.rem(lax.div(g, 4), 2), lax.div(g, 8)
    p, h = lax.div(x, 2), lax.rem(x, 2)

    def dev(q_, yh_, x_, z_, c_):
        return (q_ * 2 + c_, z_ * 8 + yh_ * 4 + x_)

    def group_peer(i):
        q_ = lax.rem(q + (i // 4), 4)
        yh_ = lax.rem(yh + (i // 2) % 2, 2)
        h_ = lax.rem(h + i % 2, 2)
        return q_, yh_, h_

    def x_peer(d):
        return dev(q, yh, lax.rem(x + d, 4), z, c)

    def q_peer(d):
        return dev(lax.rem(q + d, 4), yh, x, z, c)

    def z_peer(d):
        return dev(q, yh, x, lax.rem(z + d, 12), c)

    def y_peer(d):
        y_ = lax.rem(yh * 4 + q + d, 8)
        return dev(lax.rem(y_, 4), lax.div(y_, 4), x, z, c)

    core_peer = dev(q, yh, x, z, 1 - c)

    def remote(src, dst, s, r, to):
        return pltpu.make_async_remote_copy(
            src_ref=src, dst_ref=dst, send_sem=s, recv_sem=r, device_id=to, device_id_type=MESH
        )

    loads = [
        pltpu.make_async_copy(
            act.at[:, pl.ds(pl.multiple_of(q * 2048 + half * 1024, 1024), 1024)],
            DA.at[half, pl.ds(128, 128)],
            a_sem.at[half],
        )
        for half in range(2)
    ]
    for copy in loads:
        copy.start()

    barrier = pltpu.get_barrier_semaphore()
    count = 0
    for i in range(1, 16):
        q_, yh_, h_ = group_peer(i)
        pl.semaphore_signal(
            barrier, inc=1, device_id=dev(q_, yh_, 2 * p + h_, z, c), device_id_type=MESH
        )
        count += 1
    for d in range(1, 4):
        pl.semaphore_signal(barrier, inc=1, device_id=x_peer(d), device_id_type=MESH)
        count += 1
    for d in range(1, 12):
        pl.semaphore_signal(barrier, inc=1, device_id=z_peer(d), device_id_type=MESH)
        count += 1
    pl.semaphore_signal(barrier, inc=1, device_id=core_peer, device_id_type=MESH)
    count += 1
    pl.semaphore_wait(barrier, count)

    r_own = q * 4 + yh * 2 + h

    def piece(q_, h_):
        return w_ref.at[:, pl.ds(pl.multiple_of((q_ * 2 + h_) * 1024, 1024), 1024)]

    p0 = []
    for i in range(1, 16):
        q_, yh_, h_ = group_peer(i)
        p0.append(
            remote(
                piece(q_, h_), rbuf.at[r_own], p0_s.at[i], p0_r.at[i],
                dev(q_, yh_, 2 * p + h_, z, c),
            )
        )
    for copy in p0:
        copy.start()
    own = pltpu.make_async_copy(piece(q, h), rbuf.at[r_own], own_sem)
    own.start()

    col = lax.broadcasted_iota(jnp.int32, (96, 384), 1)
    row = lax.broadcasted_iota(jnp.int32, (96, 384), 0)
    pc = jnp.where(col >= 192, 1, 0)
    zc = (col - 192 * pc) >> 4
    rc = col & 15
    held = zc * 8 + ((rc >> 1) & 1) * 4 + pc * 2 + (rc & 1)
    hot[...] = jnp.where((held == row) & ((rc >> 2) == q), 1.0, 0.0).astype(bf16)
    bias8 = jnp.broadcast_to(bias_ref[...], (8, 96))
    bias_wide = sum(nn(part, hot[...]) for part in split3(bias8))[0:1, :]

    own.wait()
    for copy in p0:
        copy.wait_recv()
    W[h, p, z] = jnp.concatenate([rbuf[i] for i in range(16)], axis=0).astype(bf16)

    def block(j, z_):
        x_ = lax.rem(x + j, 4)
        return W.at[lax.rem(x_, 2), lax.div(x_, 2), lax.rem(z_ + 12, 12)]

    agx = [
        remote(block(0, z), block(0, z), agx_s.at[d], agx_r.at[d], x_peer(d)) for d in range(1, 4)
    ]
    for copy in agx:
        copy.start()

    def right(k, j):
        b = block(j, z - k)
        return remote(b, b, right_s.at[k, j], right_r.at[k, j], z_peer(1))

    def left(k, j):
        b = block(j, z + k)
        return remote(b, b, left_s.at[k, j], left_r.at[k, j], z_peer(11))

    def wait_right(k, j):
        b = block(j, z - k - 1)
        remote(b, b, right_s.at[k, j], right_r.at[k, j], z_peer(1)).wait_recv()

    def wait_left(k, j):
        b = block(j, z + k + 1)
        remote(b, b, left_s.at[k, j], left_r.at[k, j], z_peer(11)).wait_recv()

    for j in (0, 1, 3, 2):
        if j:
            b = block(j, z)
            remote(b, b, agx_s.at[4 - j], agx_r.at[4 - j], x_peer(4 - j)).wait_recv()
        right(0, j).start()
        left(0, j).start()

    @pl.loop(1, 5)
    def _(k):
        for j in (0, 1, 3, 2):
            wait_right(k - 1, j)
            right(k, j).start()
            wait_left(k - 1, j)
            left(k, j).start()

    for j in (0, 1, 3, 2):
        wait_right(4, j)
        right(5, j).start()
    for j in (0, 1, 3, 2):
        wait_left(4, j)
    for j in (0, 1, 3, 2):
        wait_right(5, j)

    for copy in loads:
        copy.wait()

    def rows(half):
        return W[half].reshape(384, 1024)

    pre_part = nt(DA[0, 128:256], rows(0)) + nt(DA[1, 128:256], rows(1)) + bias_wide
    pq[...] = pre_part.reshape(4, 32, 384)
    pre_send = []
    for d in (2, 1, 3):
        pre_send.append(
            remote(pq.at[lax.rem(q + d, 4)], pr.at[d], pre_s.at[d], pre_r.at[d], q_peer(d))
        )
    for copy in pre_send:
        copy.start()

    ones = jnp.ones((8, 1024), bf16)
    squares = jnp.zeros((8, 384), f32)
    for half in range(2):
        wide = rows(half).astype(f32)
        sq = wide * wide
        hi = sq.astype(bf16)
        low = (sq - hi.astype(f32)).astype(bf16)
        squares = squares + nt(ones, hi) + nt(ones, low)
    for s in range(4):
        dq[s, 32:40] = squares

    for copy in pre_send:
        copy.wait_recv()
    pre = (pq[q] + pr[1]) + (pr[2] + pr[3])
    codes = jnp.maximum(pre, 0.0)
    C[q] = codes.astype(bf16)
    code_send = [
        remote(C.at[q], C.at[q], code_s.at[d], code_r.at[d], q_peer(d)) for d in (2, 1, 3)
    ]
    for copy in code_send:
        copy.start()
    for d in (1, 3, 2):
        b = C.at[lax.rem(q + 4 - d, 4)]
        remote(b, b, code_s.at[d], code_r.at[d], q_peer(d)).wait_recv()
    codes_low = C[...].reshape(128, 384)

    core_send = []
    for half in range(2):
        part = nn(codes_low, rows(half))
        rown[half] = part
        rs[half] = part.astype(bf16)
        copy = remote(rs.at[half], rr.at[half], core_s.at[half], core_r.at[half], core_peer)
        copy.start()
        core_send.append(copy)
    codes_t = jnp.transpose(codes_low.astype(f32)).astype(bf16)
    LT[0, :, 0:128] = codes_t[0:192]
    LT[1, :, 0:128] = codes_t[192:384]
    squared = jnp.zeros((1, 128), f32)
    dcode_part = jnp.zeros((128, 384), f32)
    for half in range(2):
        core_send[half].wait_recv()
        for t in range(4):
            at = slice(t * 32, t * 32 + 32)
            error = (rown[half, at] + rr[half, at].astype(f32)) - DA[
                half, 128 + t * 32 : 160 + t * 32
            ].astype(f32)
            DA[half, at] = (error * (2.0 / TOKENS)).astype(bf16)
            squared = squared + fold(jnp.sum(error * error, axis=0, keepdims=True))
        dcode_part = dcode_part + nt(DA[half, 0:128], rows(half))
    for s in range(4):
        dq[s, 0:32] = dcode_part[s * 32 : s * 32 + 32]
    dc_send = []
    for d in (2, 1, 3):
        dc_send.append(
            remote(dq.at[lax.rem(q + d, 4)], dr.at[d], dc_s.at[d], dc_r.at[d], q_peer(d))
        )
    for copy in dc_send:
        copy.start()
    for copy in dc_send:
        copy.wait_recv()
    dcode = (dq[q] + dr[1]) + (dr[2] + dr[3])
    norms = jnp.sqrt(dcode[32:33] + 1e-6)
    dcode = dcode[0:32] + (sparsity / TOKENS) * norms
    dpre = jnp.where(pre > 0, dcode, 0.0)
    E[q] = dpre.astype(bf16)
    dp_send = [remote(E.at[q], E.at[q], dp_s.at[d], dp_r.at[d], q_peer(d)) for d in (2, 1, 3)]
    for copy in dp_send:
        copy.start()

    bias_part = jnp.sum(dpre, axis=0, keepdims=True)
    counts = jnp.sum(codes, axis=0, keepdims=True)
    loss_part = 0.5 * squared + sparsity * fold(counts * norms)
    vx[x] = jnp.concatenate(
        [bias_part[:, i * 128 : i * 128 + 128] for i in range(3)]
        + [counts[:, i * 128 : i * 128 + 128] for i in range(3)]
        + [loss_part, jnp.zeros((1, 128), f32)],
        axis=0,
    )
    vx_send = [remote(vx.at[x], vx.at[x], vx_s.at[d], vx_r.at[d], x_peer(d)) for d in range(1, 4)]
    for copy in vx_send:
        copy.start()

    for d in (1, 3, 2):
        b = E.at[lax.rem(q + 4 - d, 4)]
        remote(b, b, dp_s.at[d], dp_r.at[d], q_peer(d)).wait_recv()
    dpre_t = jnp.transpose(E[...].reshape(128, 384).astype(f32)).astype(bf16)
    LT[0, :, 128:256] = dpre_t[0:192]
    LT[1, :, 128:256] = dpre_t[192:384]

    for j in (2, 1, 3, 0):
        x_ = lax.rem(x + j, 4)
        part = nn(LT[lax.div(x_, 2)], DA[lax.rem(x_, 2)])
        gs[j] = part.astype(bf16).reshape(12, 16, 1024)

    def order(i):
        k = 6 + (1 - 2 * lax.rem(i, 2)) * lax.div(i + 1, 2)
        return k, lax.rem(z + k, 12)

    def gx(i, j):
        k, z_ = order(i)
        return remote(gs.at[j, z_], gr.at[j, z_], gx_s.at[j, i], gx_r.at[j, i], x_peer(j))

    @pl.loop(0, 12)
    def _(i):
        for j in (2, 1, 3):
            gx(i, j).start()

    for d in range(1, 4):
        b = vx.at[lax.rem(x + 4 - d, 4)]
        remote(b, b, vx_s.at[d], vx_r.at[d], x_peer(d)).wait_recv()
    y = yh * 4 + q
    vy[y] = (vx[0] + vx[1]) + (vx[2] + vx[3])
    vy_send = [remote(vy.at[y], vy.at[y], vy_s.at[d], vy_r.at[d], y_peer(d)) for d in range(1, 8)]
    for copy in vy_send:
        copy.start()

    def reduce_x(i):
        k, z_ = order(i)
        for j in (1, 3, 2):
            gx(i, j).wait_recv()
        return (gs[0, z_].astype(f32) + gr[1, z_].astype(f32)) + (
            gr[2, z_].astype(f32) + gr[3, z_].astype(f32)
        )

    def gz(k):
        return remote(hs.at[k], hr.at[k], gz_s.at[k], gz_r.at[k], z_peer(k))

    def send_z(i):
        k, _ = order(i)
        hs[k] = reduce_x(i).astype(bf16)
        gz(k).start()

    @pl.loop(0, 6)
    def _(i):
        send_z(i)

    for d in range(1, 8):
        b = vy.at[lax.rem(y + 8 - d, 8)]
        remote(b, b, vy_s.at[d], vy_r.at[d], y_peer(d)).wait_recv()
    v = vy[0]
    for i in range(1, 8):
        v = v + vy[i]
    vz[z] = v
    vz_send = [remote(vz.at[z], vz.at[z], vz_s.at[d], vz_r.at[d], z_peer(d)) for d in range(1, 12)]
    for copy in vz_send:
        copy.start()

    @pl.loop(6, 11)
    def _(i):
        send_z(i)

    hown[...] = reduce_x(11)

    for d in range(1, 12):
        b = vz.at[lax.rem(z + 12 - d, 12)]
        remote(b, b, vz_s.at[d], vz_r.at[d], z_peer(d)).wait_recv()
    v = vz[0]
    for i in range(1, 12):
        v = v + vz[i]
    vc[0] = v
    vc_send = remote(vc.at[0], vc.at[1], vc_s.at[0], vc_r.at[0], core_peer)
    vc_send.start()

    @pl.loop(0, 11)
    def _(i):
        k, _ = order(i)
        gz(k).wait_recv()
        hown[...] += hr[k].astype(f32)

    total = hown[...]
    for i in range(16):
        fs[i] = total[i : i + 1]
    slot = (q * 2 + h) * 2 + yh
    fin = []
    for i in range(1, 16):
        q_, yh_, h_ = group_peer(i)
        fin.append(
            remote(
                fs.at[q_ * 4 + yh_ * 2 + h_], fr.at[slot], fin_s.at[i], fin_r.at[i],
                dev(q_, yh_, 2 * p + h_, z, c),
            )
        )
    for copy in fin:
        copy.start()
    fr[slot] = fs[r_own]

    bias8 = jnp.concatenate([v[0:1], v[1:2], v[2:3]], axis=1)
    bias8 = jnp.broadcast_to(bias8, (8, 384))
    bias_grad = sum(nt(part, hot[...]) for part in split3(bias8))[0:1, :]
    index = p * 192 + z * 16 + r_own
    lane = lax.broadcasted_iota(jnp.int32, (1, 128), 1)
    mine = jnp.zeros((1, 128), f32)
    for i in range(3):
        mine = mine + jnp.where(lane + i * 128 == index, v[3 + i : 4 + i], 0.0)
    my_count = jnp.sum(mine, axis=1, keepdims=True)
    vc_send.wait_recv()
    loss = jnp.sum(v[6:7] + vc[1, 6:7], axis=1, keepdims=True) * (1.0 / TOKENS)
    small_ref[...] = jnp.zeros((8, 128), f32)
    small_ref[0:1, 0:96] = bias_grad
    small_ref[1:2, :] = jnp.broadcast_to(loss, (1, 128))

    own_row = w_ref[...].astype(bf16).astype(f32)
    own_norm = jnp.sqrt(jnp.sum(own_row * own_row, axis=1, keepdims=True) + 1e-6)
    scale = (sparsity / TOKENS) * my_count / own_norm
    for copy in fin:
        copy.wait_recv()
    for s in range(8):
        at = slice(s * 1024, s * 1024 + 1024)
        grad_ref[:, at] = (fr[2 * s] + fr[2 * s + 1]) + scale * own_row[:, at]

    for copy in p0 + agx + pre_send + code_send + core_send + dc_send + dp_send + fin:
        copy.wait_send()
    for copy in vx_send + vy_send + vz_send + [vc_send]:
        copy.wait_send()

    @pl.loop(0, 5)
    def _(k):
        for j in range(4):
            right(k, j).wait_send()
            left(k, j).wait_send()

    for j in range(4):
        right(5, j).wait_send()

    @pl.loop(0, 12)
    def _(i):
        for j in (1, 2, 3):
            gx(i, j).wait_send()

    @pl.loop(1, 12)
    def _(k):
        gz(k).wait_send()


def step(activations, weight, code_bias):
    dma = pltpu.SemaphoreType.DMA
    vmem = pltpu.VMEM
    return pl.pallas_call(
        kernel,
        out_shape=(
            jax.ShapeDtypeStruct((1, 8192), f32),
            jax.ShapeDtypeStruct((8, 128), f32),
        ),
        in_specs=[
            pl.BlockSpec(memory_space=pl.ANY),
            pl.BlockSpec(memory_space=pltpu.VMEM),
            pl.BlockSpec(memory_space=pltpu.VMEM),
        ],
        out_specs=[pl.BlockSpec(memory_space=pltpu.VMEM)] * 2,
        scratch_shapes=[
            vmem((16, 1, 1024), f32),
            vmem((2, 2, 12, 16, 1024), bf16),
            vmem((2, 256, 1024), bf16),
            vmem((2, 192, 256), bf16),
            vmem((4, 32, 384), f32),
            vmem((4, 32, 384), f32),
            vmem((4, 32, 384), bf16),
            vmem((2, 128, 1024), f32),
            vmem((2, 128, 1024), bf16),
            vmem((2, 128, 1024), bf16),
            vmem((4, 40, 384), f32),
            vmem((4, 40, 384), f32),
            vmem((4, 32, 384), bf16),
            vmem((4, 12, 16, 1024), bf16),
            vmem((4, 12, 16, 1024), bf16),
            vmem((12, 16, 1024), bf16),
            vmem((12, 16, 1024), bf16),
            vmem((16, 1024), f32),
            vmem((16, 1, 1024), f32),
            vmem((16, 1, 1024), f32),
            vmem((4, 8, 128), f32),
            vmem((8, 8, 128), f32),
            vmem((12, 8, 128), f32),
            vmem((2, 8, 128), f32),
            vmem((96, 384), bf16),
            dma((2,)),
            dma,
            dma((16,)), dma((16,)),
            dma((4,)), dma((4,)),
            dma((6, 4)), dma((6, 4)),
            dma((5, 4)), dma((5, 4)),
            dma((4,)), dma((4,)),
            dma((4,)), dma((4,)),
            dma((2,)), dma((2,)),
            dma((4,)), dma((4,)),
            dma((4,)), dma((4,)),
            dma((4, 12)), dma((4, 12)),
            dma((12,)), dma((12,)),
            dma((16,)), dma((16,)),
            dma((4,)), dma((4,)),
            dma((8,)), dma((8,)),
            dma((12,)), dma((12,)),
            dma((1,)), dma((1,)),
        ],
        compiler_params=pltpu.CompilerParams(
            collective_id=0, has_side_effects=True, vmem_limit_bytes=48 * 1024 * 1024
        ),
    )(activations, weight, code_bias.reshape(1, 96))


def per_device(activations, weight, weight_mean, weight_square, code_bias, bias_mean, bias_square):
    grad_own, small = step(activations, weight, code_bias)
    bias_grad = small[0, :96]
    total_loss = small[1, 0]
    after_weight, after_mean, after_square = adam_step(weight, weight_mean, weight_square, grad_own)
    after_bias, after_biasmean, after_biassquare = adam_step(
        code_bias, bias_mean, bias_square, bias_grad
    )
    return (
        after_weight,
        after_mean,
        after_square,
        after_bias,
        after_biasmean,
        after_biassquare,
        total_loss,
    )


def solution(mesh):
    placed = (
        P("dp", None),
        P(("latent", "dp"), None),
        P(("latent", "dp"), None),
        P(("latent", "dp"), None),
        P("latent"),
        P("latent"),
        P("latent"),
    )
    return jax.shard_map(
        per_device,
        mesh=mesh,
        in_specs=placed,
        out_specs=(
            P(("latent", "dp"), None),
            P(("latent", "dp"), None),
            P(("latent", "dp"), None),
            P("latent"),
            P("latent"),
            P("latent"),
            P(),
        ),
        check_vma=False,
    )
```

```python
import functools

import jax
import jax.numpy as jnp
from jax import lax
from jax.experimental import pallas as pl
from jax.experimental.pallas import tpu as pltpu
from jax.sharding import PartitionSpec as P

sparsity = 2.0
first_decay = 0.9
second_decay = 0.999
learn_rate = 0.002
adam_floor = 1e-08
first_fix = 0.9999734386011124
second_fix = 0.09520785288629108

TOKENS = 12288
MESH = pl.DeviceIdType.MESH
bf16 = jnp.bfloat16
f32 = jnp.float32


def adam_step(value, mean, square, grad):
    mean_new = first_decay * mean + (1.0 - first_decay) * grad
    square_new = second_decay * square + (1.0 - second_decay) * grad * grad
    value_new = value - learn_rate * (mean_new / first_fix) / (
        jnp.sqrt(square_new / second_fix) + adam_floor
    )
    return (value_new, mean_new, square_new)


def split3(v):
    hi = v.astype(bf16)
    rest = v - hi.astype(f32)
    mid = rest.astype(bf16)
    low = (rest - mid.astype(f32)).astype(bf16)
    return hi, mid, low


def nt(a, b):
    return lax.dot_general(a, b, (((1,), (1,)), ((), ())), preferred_element_type=f32)


def nn(a, b):
    return jnp.dot(a, b, preferred_element_type=f32)


def fold(v):
    total = v[:, 0:128]
    for i in range(1, v.shape[1] // 128):
        total = total + v[:, i * 128 : (i + 1) * 128]
    return total


def slot(dz):
    if dz == 6:
        return 11
    return -2 * dz - 1 if dz < 0 else 2 * dz


KINDS = ((0, 1), (1, 1), (1, 0))
CHUNKS = ((0, 8), (8, 12))


def kernel(
    act, w_any, b_any, grad_ref, small_ref,
    wv, bv, rbuf, W, DA, LT, pqa, pqb, pra, prb, ca, cb, rown, rs, rr,
    dqa, dqb, dra, drb, ea, eb, gs, gr, hs, hr, hown, fs, fr,
    vx, vy, vz, vc, hot, turn,
    a_sem, own_sem,
    p0_s, p0_r, ax_s, ax_r, ad_s, ad_r, az_s, az_r,
    pre_s, pre_r, code_s, code_r, core_s, core_r, dc_s, dc_r, dp_s, dp_r,
    gx_s, gx_r, gz_s, gz_r, fin_s, fin_r, vx_s, vx_r, vy_s, vy_r, vz_s, vz_r, vc_s, vc_r,
):
    l = lax.axis_index("latent")
    g = lax.axis_index("dp")
    q, c = lax.div(l, 2), lax.rem(l, 2)
    x, yh, z = lax.rem(g, 4), lax.rem(lax.div(g, 4), 2), lax.div(g, 8)
    p, h = lax.div(x, 2), lax.rem(x, 2)

    def dev(q_, yh_, x_, z_, c_):
        return (q_ * 2 + c_, z_ * 8 + yh_ * 4 + x_)

    def group_peer(i):
        q_ = lax.rem(q + (i // 4), 4)
        yh_ = lax.rem(yh + (i // 2) % 2, 2)
        h_ = lax.rem(h + i % 2, 2)
        return q_, yh_, h_

    def flip(bit, by):
        return 1 - bit if by else bit

    def kind_peer(kind):
        half, pair = KINDS[kind]
        return dev(q, yh, 2 * flip(p, pair) + flip(h, half), z, c)

    def x_peer(d):
        return dev(q, yh, lax.rem(x + d, 4), z, c)

    def q_peer(d):
        return dev(lax.rem(q + d, 4), yh, x, z, c)

    def z_peer(d):
        return dev(q, yh, x, lax.rem(z + d + 12, 12), c)

    def y_peer(d):
        y_ = lax.rem(yh * 4 + q + d, 8)
        return dev(lax.rem(y_, 4), lax.div(y_, 4), x, z, c)

    core_peer = dev(q, yh, x, z, 1 - c)
    started = []

    def remote(src, dst, s, r, to):
        return pltpu.make_async_remote_copy(
            src_ref=src, dst_ref=dst, send_sem=s, recv_sem=r, device_id=to, device_id_type=MESH
        )

    def start(copy):
        copy.start()
        started.append(copy.wait_send)

    barrier = pltpu.get_barrier_semaphore()
    peers = []
    for i in range(1, 16):
        q_, yh_, h_ = group_peer(i)
        peers.append(dev(q_, yh_, 2 * p + h_, z, c))
    peers += [kind_peer(0), kind_peer(1)] + [z_peer(d) for d in range(1, 12)] + [core_peer]
    for peer in peers:
        pl.semaphore_signal(barrier, inc=1, device_id=peer, device_id_type=MESH)

    loads = [
        pltpu.make_async_copy(
            act.at[:, pl.ds(pl.multiple_of(q * 2048 + flip(h, half) * 1024, 1024), 1024)],
            DA.at[half, pl.ds(128, 128)],
            a_sem.at[half],
        )
        for half in range(2)
    ]
    small_loads = [
        pltpu.make_async_copy(w_any, wv, a_sem.at[2]),
        pltpu.make_async_copy(b_any, bv, a_sem.at[3]),
    ]
    for copy in small_loads + loads:
        copy.start()

    pl.semaphore_wait(barrier, len(peers))

    r_own = q * 4 + yh * 2 + h

    def piece(q_, h_):
        return w_any.at[:, pl.ds(pl.multiple_of((q_ * 2 + h_) * 1024, 1024), 1024)]

    p0 = []
    for i in range(1, 16):
        q_, yh_, h_ = group_peer(i)
        p0.append(
            remote(
                piece(q_, h_), rbuf.at[r_own], p0_s.at[i], p0_r.at[i],
                dev(q_, yh_, 2 * p + h_, z, c),
            )
        )
    for copy in p0:
        start(copy)
    own = pltpu.make_async_copy(piece(q, h), rbuf.at[r_own], own_sem)
    own.start()

    def place(at):
        near, pair, r = at >> 5, (at >> 4) & 1, at & 15
        far = (near + 1) >> 1
        z_ = z + jnp.where((near & 1) == 1, -far, far)
        z_ = jnp.where(z_ < 0, z_ + 12, jnp.where(z_ >= 12, z_ - 12, z_))
        x_ = 2 * (p + pair - 2 * p * pair) + (r & 1)
        return (r >> 2) * 96 + z_ * 8 + ((r >> 1) & 1) * 4 + x_

    col = lax.broadcasted_iota(jnp.int32, (96, 384), 1)
    row = lax.broadcasted_iota(jnp.int32, (96, 384), 0)
    hot[...] = jnp.where(place(col) == q * 96 + row, 1.0, 0.0).astype(bf16)
    held = place(lax.broadcasted_iota(jnp.int32, (384, 128), 0))
    for i in range(3):
        to = lax.broadcasted_iota(jnp.int32, (384, 128), 1) + i * 128
        turn[:, i * 128 : i * 128 + 128] = jnp.where(held == to, 1.0, 0.0).astype(bf16)
    for copy in small_loads:
        copy.wait()
    bias8 = jnp.broadcast_to(bv[...], (8, 96))
    bias_wide = sum(nn(part, hot[...]) for part in split3(bias8))[0:1, :]
    own.wait()
    for copy in p0:
        copy.wait_recv()
    W[0, 0, 0] = jnp.concatenate([rbuf[i] for i in range(16)], axis=0).astype(bf16)

    def az(t, dz, s):
        to = slot(dz - s) if dz - s != -6 else 11
        return remote(
            W.at[0, slot(dz), t], W.at[0, to, t], az_s.at[t, to], az_r.at[t, to], z_peer(s)
        )

    def wait_z(t, dz):
        b = W.at[0, slot(dz), t]
        remote(b, b, az_s.at[t, slot(dz)], az_r.at[t, slot(dz)], z_peer(1)).wait_recv()

    def ax(kind, dz):
        at = slot(dz)
        return remote(
            W.at[0, at, 0], W.at[1, at, KINDS[kind][1]], ax_s.at[kind, at], ax_r.at[kind, at],
            kind_peer(kind),
        )

    def along_x(dz):
        start(ax(1, dz))
        start(ax(2, dz))

    def wait_x(dz):
        ax(1, dz).wait_recv()
        ax(2, dz).wait_recv()

    def onward(t, dz):
        for way in ((1, -1) if dz == 0 else (1,) if dz < 0 else (-1,)):
            for hops in (2, 1):
                if abs(dz) + hops == 6 and (dz < 0) == (t == 1):
                    continue
                start(az(t, dz, way * hops))

    two = remote(W.at[0, 0, 0], W.at[0, 0, 1], ad_s, ad_r, kind_peer(0))
    start(two)
    onward(0, 0)
    along_x(0)
    two.wait_recv()
    onward(1, 0)
    for dz in (-2, 2):
        wait_z(0, dz)
        onward(0, dz)
        along_x(dz)
    for dz in (-1, 1):
        wait_z(0, dz)
        along_x(dz)
    for dz in (-2, 2):
        wait_z(1, dz)
        onward(1, dz)
    for dz in (-4, 4):
        wait_z(0, dz)
        onward(0, dz)
        along_x(dz)
    for dz in (-3, 3):
        wait_z(0, dz)
        along_x(dz)
    for dz in (-4, 4):
        wait_z(1, dz)
        onward(1, dz)
    for copy in loads:
        copy.wait()

    def rows(half, chunk):
        first, last = CHUNKS[chunk]
        return W[half, first:last].reshape(32 * (last - first), 1024)

    def lanes(chunk):
        first, last = CHUNKS[chunk]
        return slice(32 * first, 32 * last)

    pq, pr, C = (pqa, pqb), (pra, prb), (ca, cb)
    dq, dr, E = (dqa, dqb), (dra, drb), (ea, eb)

    def to_slabs(send, recv, chunk, s, r):
        copies = [
            remote(send.at[lax.rem(q + d, 4)], recv.at[d], s.at[chunk, d], r.at[chunk, d], q_peer(d))
            for d in (2, 1, 3)
        ]
        for copy in copies:
            start(copy)
        return copies

    def share(buffer, chunk, s, r):
        for d in (2, 1, 3):
            start(
                remote(buffer.at[q], buffer.at[q], s.at[chunk, d], r.at[chunk, d], q_peer(d))
            )

    def shared(buffer, chunk, s, r):
        for d in (1, 3, 2):
            b = buffer.at[lax.rem(q + 4 - d, 4)]
            remote(b, b, s.at[chunk, d], r.at[chunk, d], q_peer(d)).wait_recv()
        return buffer[...].reshape(128, buffer.shape[2])

    def make_pre(chunk):
        part = nt(DA[0, 128:256], rows(0, chunk)) + nt(DA[1, 128:256], rows(1, chunk))
        part = part + bias_wide[:, lanes(chunk)]
        pq[chunk][...] = part.reshape(4, 32, part.shape[1])
        return to_slabs(pq[chunk], pr[chunk], chunk, pre_s, pre_r)

    def make_codes(chunk, copies):
        for copy in copies:
            copy.wait_recv()
        s, r = pq[chunk], pr[chunk]
        pre = (s[q] + r[1]) + (r[2] + r[3])
        codes = jnp.maximum(pre, 0.0)
        C[chunk][q] = codes.astype(bf16)
        share(C[chunk], chunk, code_s, code_r)
        return pre, codes

    for dz in (0, -1, 1, -2, 2, -3, 3, -4):
        wait_x(dz)
    for dz in (-1, 1, -3, 3):
        wait_z(1, dz)
    copies_a = make_pre(0)
    for dz in (-5, 5, 6):
        wait_z(0, dz)
        along_x(dz)
    for dz in (-5, 5, 6):
        wait_z(1, dz)
    for dz in (4, -5, 5, 6):
        wait_x(dz)
    copies_b = make_pre(1)
    pre_a, codes_a = make_codes(0, copies_a)

    ones = jnp.ones((8, 1024), bf16)
    for chunk in range(2):
        squares = None
        for half in range(2):
            wide = rows(half, chunk).astype(f32)
            sq = wide * wide
            hi = sq.astype(bf16)
            low = (sq - hi.astype(f32)).astype(bf16)
            part = nt(ones, hi) + nt(ones, low)
            squares = part if squares is None else squares + part
        for s in range(4):
            dq[chunk][s, 32:40] = squares

    pre_b, codes_b = make_codes(1, copies_b)
    low = [shared(C[chunk], chunk, code_s, code_r) for chunk in range(2)]

    core_send = []
    for half in range(2):
        part = nn(low[0], rows(half, 0)) + nn(low[1], rows(half, 1))
        rown[half] = part
        rs[half] = part.astype(bf16)
        copy = remote(rs.at[half], rr.at[half], core_s.at[half], core_r.at[half], core_peer)
        start(copy)
        core_send.append(copy)
    for chunk in range(2):
        LT[lanes(chunk), 0:128] = jnp.transpose(low[chunk].astype(f32)).astype(bf16)
    squared = jnp.zeros((1, 128), f32)
    for half in range(2):
        core_send[half].wait_recv()
        for t in range(4):
            at = slice(t * 32, t * 32 + 32)
            error = (rown[half, at] + rr[half, at].astype(f32)) - DA[
                half, 128 + t * 32 : 160 + t * 32
            ].astype(f32)
            DA[half, at] = (error * (2.0 / TOKENS)).astype(bf16)
            squared = squared + fold(jnp.sum(error * error, axis=0, keepdims=True))

    def make_dcode(chunk):
        part = nt(DA[0, 0:128], rows(0, chunk)) + nt(DA[1, 0:128], rows(1, chunk))
        for s in range(4):
            dq[chunk][s, 0:32] = part[s * 32 : s * 32 + 32]
        return to_slabs(dq[chunk], dr[chunk], chunk, dc_s, dc_r)

    def make_dpre(chunk, copies, pre):
        for copy in copies:
            copy.wait_recv()
        s, r = dq[chunk], dr[chunk]
        dcode = (s[q] + r[1]) + (r[2] + r[3])
        norms = jnp.sqrt(dcode[32:33] + 1e-6)
        dpre = jnp.where(pre > 0, dcode[0:32] + (sparsity / TOKENS) * norms, 0.0)
        E[chunk][q] = dpre.astype(bf16)
        share(E[chunk], chunk, dp_s, dp_r)
        return dpre, norms

    dcode_b = make_dcode(1)
    dcode_a = make_dcode(0)
    dpre_b, norms_b = make_dpre(1, dcode_b, pre_b)
    dpre_a, norms_a = make_dpre(0, dcode_a, pre_a)

    def make_grad(chunk):
        first, last = CHUNKS[chunk]
        dpre_low = shared(E[chunk], chunk, dp_s, dp_r)
        LT[lanes(chunk), 128:256] = jnp.transpose(dpre_low.astype(f32)).astype(bf16)
        for half in range(2):
            part = nn(LT[lanes(chunk)], DA[half])
            gs[half, first:last] = part.astype(bf16).reshape(last - first, 2, 16, 1024)

    def gx(at, kind):
        half, pair = KINDS[kind]
        return remote(
            gs.at[half, at, pair], gr.at[kind, at], gx_s.at[kind, at], gx_r.at[kind, at],
            kind_peer(kind),
        )

    make_grad(1)

    @pl.loop(0, 4)
    def _(i):
        for kind in range(3):
            gx(11 - i, kind).start()

    bias_part = jnp.concatenate(
        [jnp.sum(v, axis=0, keepdims=True) for v in (dpre_a, dpre_b)], axis=1
    )
    counts = jnp.concatenate(
        [jnp.sum(v, axis=0, keepdims=True) for v in (codes_a, codes_b)], axis=1
    )
    norms = jnp.concatenate([norms_a, norms_b], axis=1)
    loss_part = 0.5 * squared + sparsity * fold(counts * norms)
    both = jnp.concatenate([bias_part, counts, jnp.zeros((6, 384), f32)], axis=0)
    both = sum(nn(part, turn[...]) for part in split3(both))
    vx[x] = jnp.concatenate(
        [both[0:1, i * 128 : i * 128 + 128] for i in range(3)]
        + [both[1:2, i * 128 : i * 128 + 128] for i in range(3)]
        + [loss_part, jnp.zeros((1, 128), f32)],
        axis=0,
    )
    for d in range(1, 4):
        start(remote(vx.at[x], vx.at[x], vx_s.at[d], vx_r.at[d], x_peer(d)))

    make_grad(0)

    @pl.loop(4, 12)
    def _(i):
        for kind in range(3):
            gx(11 - i, kind).start()

    for done in started:
        done()
    started.clear()

    def x_sent():
        @pl.loop(0, 12)
        def _(i):
            for kind in range(3):
                gx(i, kind).wait_send()

    started.append(x_sent)

    for d in range(1, 4):
        b = vx.at[lax.rem(x + 4 - d, 4)]
        remote(b, b, vx_s.at[d], vx_r.at[d], x_peer(d)).wait_recv()
    y = yh * 4 + q
    vy[y] = (vx[0] + vx[1]) + (vx[2] + vx[3])
    for d in range(1, 8):
        start(remote(vy.at[y], vy.at[y], vy_s.at[d], vy_r.at[d], y_peer(d)))

    def reduce_x(at):
        for kind in (1, 2, 0):
            gx(at, kind).wait_recv()
        return (gs[0, at, 0].astype(f32) + gr[0, at].astype(f32)) + (
            gr[1, at].astype(f32) + gr[2, at].astype(f32)
        )

    def gz(at):
        far = lax.div(at + 1, 2)
        dz = (1 - 2 * lax.rem(at, 2)) * far
        return remote(hs.at[at], hr.at[at], gz_s.at[at], gz_r.at[at], z_peer(dz))

    def send_z(at):
        hs[at] = reduce_x(at).astype(bf16)
        gz(at).start()

    @pl.loop(0, 5)
    def _(i):
        send_z(11 - i)

    for d in range(1, 8):
        b = vy.at[lax.rem(y + 8 - d, 8)]
        remote(b, b, vy_s.at[d], vy_r.at[d], y_peer(d)).wait_recv()
    v = vy[0]
    for i in range(1, 8):
        v = v + vy[i]
    vz[z] = v
    for d in range(1, 12):
        start(remote(vz.at[z], vz.at[z], vz_s.at[d], vz_r.at[d], z_peer(d)))

    @pl.loop(5, 11)
    def _(i):
        send_z(11 - i)

    def z_sent():
        @pl.loop(1, 12)
        def _(k):
            gz(k).wait_send()

    started.append(z_sent)
    hown[...] = reduce_x(0)

    for d in range(1, 12):
        b = vz.at[lax.rem(z + 12 - d, 12)]
        remote(b, b, vz_s.at[d], vz_r.at[d], z_peer(d)).wait_recv()
    v = vz[0]
    for i in range(1, 12):
        v = v + vz[i]
    vc[0] = v
    vc_send = remote(vc.at[0], vc.at[1], vc_s.at[0], vc_r.at[0], core_peer)
    start(vc_send)

    @pl.loop(0, 11)
    def _(i):
        gz(11 - i).wait_recv()
        hown[...] += hr[11 - i].astype(f32)

    total = hown[...]
    for i in range(16):
        fs[i] = total[i : i + 1]
    mine = (q * 2 + h) * 2 + yh
    fin = []
    for i in range(1, 16):
        q_, yh_, h_ = group_peer(i)
        fin.append(
            remote(
                fs.at[q_ * 4 + yh_ * 2 + h_], fr.at[mine], fin_s.at[i], fin_r.at[i],
                dev(q_, yh_, 2 * p + h_, z, c),
            )
        )
    for copy in fin:
        start(copy)
    fr[mine] = fs[r_own]

    bias8 = jnp.concatenate([v[0:1], v[1:2], v[2:3]], axis=1)
    bias8 = jnp.broadcast_to(bias8, (8, 384))
    pick = jnp.where(col == q * 96 + row, 1.0, 0.0).astype(bf16)
    bias_grad = sum(nt(part, pick) for part in split3(bias8))[0:1, :]
    lane = lax.broadcasted_iota(jnp.int32, (1, 128), 1)
    own_count = jnp.zeros((1, 128), f32)
    for i in range(3):
        own_count = own_count + jnp.where(lane + i * 128 == q * 96 + g, v[3 + i : 4 + i], 0.0)
    own_count = jnp.sum(own_count, axis=1, keepdims=True)
    vc_send.wait_recv()
    loss = jnp.sum(v[6:7] + vc[1, 6:7], axis=1, keepdims=True) * (1.0 / TOKENS)
    small_ref[...] = jnp.zeros((8, 128), f32)
    small_ref[0:1, 0:96] = bias_grad
    small_ref[1:2, :] = jnp.broadcast_to(loss, (1, 128))

    for done in started[:-15]:
        done()
    own_row = wv[...].astype(bf16).astype(f32)
    own_norm = jnp.sqrt(jnp.sum(own_row * own_row, axis=1, keepdims=True) + 1e-6)
    scale = (sparsity / TOKENS) * own_count / own_norm
    for copy in fin:
        copy.wait_recv()
    for s in range(8):
        at = slice(s * 1024, s * 1024 + 1024)
        grad_ref[:, at] = (fr[2 * s] + fr[2 * s + 1]) + scale * own_row[:, at]

    for done in started[-15:]:
        done()


def step(activations, weight, code_bias):
    dma = pltpu.SemaphoreType.DMA
    vmem = pltpu.VMEM
    return pl.pallas_call(
        kernel,
        out_shape=(
            jax.ShapeDtypeStruct((1, 8192), f32),
            jax.ShapeDtypeStruct((8, 128), f32),
        ),
        in_specs=[pl.BlockSpec(memory_space=pl.ANY)] * 3,
        out_specs=[pl.BlockSpec(memory_space=pltpu.VMEM)] * 2,
        scratch_shapes=[
            vmem((1, 8192), f32),
            vmem((1, 96), f32),
            vmem((16, 1, 1024), f32),
            vmem((2, 12, 2, 16, 1024), bf16),
            vmem((2, 256, 1024), bf16),
            vmem((384, 256), bf16),
            vmem((4, 32, 256), f32), vmem((4, 32, 128), f32),
            vmem((4, 32, 256), f32), vmem((4, 32, 128), f32),
            vmem((4, 32, 256), bf16), vmem((4, 32, 128), bf16),
            vmem((2, 128, 1024), f32),
            vmem((2, 128, 1024), bf16),
            vmem((2, 128, 1024), bf16),
            vmem((4, 40, 256), f32), vmem((4, 40, 128), f32),
            vmem((4, 40, 256), f32), vmem((4, 40, 128), f32),
            vmem((4, 32, 256), bf16), vmem((4, 32, 128), bf16),
            vmem((2, 12, 2, 16, 1024), bf16),
            vmem((3, 12, 16, 1024), bf16),
            vmem((12, 16, 1024), bf16),
            vmem((12, 16, 1024), bf16),
            vmem((16, 1024), f32),
            vmem((16, 1, 1024), f32),
            vmem((16, 1, 1024), f32),
            vmem((4, 8, 128), f32),
            vmem((8, 8, 128), f32),
            vmem((12, 8, 128), f32),
            vmem((2, 8, 128), f32),
            vmem((96, 384), bf16),
            vmem((384, 384), bf16),
            dma((4,)),
            dma,
            dma((16,)), dma((16,)),
            dma((3, 12)), dma((3, 12)),
            dma, dma,
            dma((2, 12)), dma((2, 12)),
            dma((2, 4)), dma((2, 4)),
            dma((2, 4)), dma((2, 4)),
            dma((2,)), dma((2,)),
            dma((2, 4)), dma((2, 4)),
            dma((2, 4)), dma((2, 4)),
            dma((3, 12)), dma((3, 12)),
            dma((12,)), dma((12,)),
            dma((16,)), dma((16,)),
            dma((4,)), dma((4,)),
            dma((8,)), dma((8,)),
            dma((12,)), dma((12,)),
            dma((1,)), dma((1,)),
        ],
        compiler_params=pltpu.CompilerParams(
            collective_id=0, has_side_effects=True, vmem_limit_bytes=52 * 1024 * 1024
        ),
    )(activations, weight, code_bias.reshape(1, 96))


def per_device(activations, weight, weight_mean, weight_square, code_bias, bias_mean, bias_square):
    grad_own, small = step(activations, weight, code_bias)
    bias_grad = small[0, :96]
    total_loss = small[1, 0]
    after_weight, after_mean, after_square = adam_step(weight, weight_mean, weight_square, grad_own)
    after_bias, after_biasmean, after_biassquare = adam_step(
        code_bias, bias_mean, bias_square, bias_grad
    )
    return (
        after_weight,
        after_mean,
        after_square,
        after_bias,
        after_biasmean,
        after_biassquare,
        total_loss,
    )


def solution(mesh):
    placed = (
        P("dp", None),
        P(("latent", "dp"), None),
        P(("latent", "dp"), None),
        P(("latent", "dp"), None),
        P("latent"),
        P("latent"),
        P("latent"),
    )
    return jax.shard_map(
        per_device,
        mesh=mesh,
        in_specs=placed,
        out_specs=(
            P(("latent", "dp"), None),
            P(("latent", "dp"), None),
            P(("latent", "dp"), None),
            P("latent"),
            P("latent"),
            P("latent"),
            P(),
        ),
        check_vma=False,
    )
```

```python
import functools

import jax
import jax.numpy as jnp
from jax import lax
from jax.experimental import pallas as pl
from jax.experimental.pallas import tpu as pltpu
from jax.sharding import PartitionSpec as P

sparsity = 2.0
first_decay = 0.9
second_decay = 0.999
learn_rate = 0.002
adam_floor = 1e-08
first_fix = 0.9999734386011124
second_fix = 0.09520785288629108

TOKENS = 12288
MESH = pl.DeviceIdType.MESH
bf16 = jnp.bfloat16
f32 = jnp.float32


def adam_step(value, mean, square, grad):
    mean_new = first_decay * mean + (1.0 - first_decay) * grad
    square_new = second_decay * square + (1.0 - second_decay) * grad * grad
    value_new = value - learn_rate * (mean_new / first_fix) / (
        jnp.sqrt(square_new / second_fix) + adam_floor
    )
    return (value_new, mean_new, square_new)


def split3(v):
    hi = v.astype(bf16)
    rest = v - hi.astype(f32)
    mid = rest.astype(bf16)
    low = (rest - mid.astype(f32)).astype(bf16)
    return hi, mid, low


def nt(a, b):
    return lax.dot_general(a, b, (((1,), (1,)), ((), ())), preferred_element_type=f32)


def nn(a, b):
    return jnp.dot(a, b, preferred_element_type=f32)


def fold(v):
    total = v[:, 0:128]
    for i in range(1, v.shape[1] // 128):
        total = total + v[:, i * 128 : (i + 1) * 128]
    return total


def slot(dz):
    if dz == 6:
        return 11
    return -2 * dz - 1 if dz < 0 else 2 * dz


KINDS = ((0, 1), (1, 1), (1, 0))
CHUNKS = ((0, 8), (8, 12))


def kernel(
    act, w_any, b_any, grad_ref, small_ref,
    wv, bv, rbuf, W, DA, LT, pqa, pqb, pra, prb, ca, cb, rown, rs, rr,
    dqa, dqb, dra, drb, ea, eb, gs, gr, hs, hr, hown, fs, fr,
    vx, vy, vz, vc, hot, turn,
    a_sem, own_sem,
    p0_s, p0_r, ax_s, ax_r, ad_s, ad_r, az_s, az_r,
    pre_s, pre_r, code_s, code_r, core_s, core_r, dc_s, dc_r, dp_s, dp_r,
    gx_s, gx_r, gz_s, gz_r, fin_s, fin_r, vx_s, vx_r, vy_s, vy_r, vz_s, vz_r, vc_s, vc_r,
):
    l = lax.axis_index("latent")
    g = lax.axis_index("dp")
    q, c = lax.div(l, 2), lax.rem(l, 2)
    x, yh, z = lax.rem(g, 4), lax.rem(lax.div(g, 4), 2), lax.div(g, 8)
    p, h = lax.div(x, 2), lax.rem(x, 2)

    def dev(q_, yh_, x_, z_, c_):
        return (q_ * 2 + c_, z_ * 8 + yh_ * 4 + x_)

    def group_peer(i):
        q_ = lax.rem(q + (i // 4), 4)
        yh_ = lax.rem(yh + (i // 2) % 2, 2)
        h_ = lax.rem(h + i % 2, 2)
        return q_, yh_, h_

    def flip(bit, by):
        return 1 - bit if by else bit

    def kind_peer(kind):
        half, pair = KINDS[kind]
        return dev(q, yh, 2 * flip(p, pair) + flip(h, half), z, c)

    def x_peer(d):
        return dev(q, yh, lax.rem(x + d, 4), z, c)

    def q_peer(d):
        return dev(lax.rem(q + d, 4), yh, x, z, c)

    def z_peer(d):
        return dev(q, yh, x, lax.rem(z + d + 12, 12), c)

    def y_peer(d):
        y_ = lax.rem(yh * 4 + q + d, 8)
        return dev(lax.rem(y_, 4), lax.div(y_, 4), x, z, c)

    core_peer = dev(q, yh, x, z, 1 - c)
    started = []

    def remote(src, dst, s, r, to):
        return pltpu.make_async_remote_copy(
            src_ref=src, dst_ref=dst, send_sem=s, recv_sem=r, device_id=to, device_id_type=MESH
        )

    def start(copy):
        copy.start()
        started.append(copy.wait_send)

    barrier = pltpu.get_barrier_semaphore()
    peers = []
    for i in range(1, 16):
        q_, yh_, h_ = group_peer(i)
        peers.append(dev(q_, yh_, 2 * p + h_, z, c))
    peers += [kind_peer(0), kind_peer(1)] + [z_peer(d) for d in range(1, 12)] + [core_peer]
    for peer in peers:
        pl.semaphore_signal(barrier, inc=1, device_id=peer, device_id_type=MESH)

    loads = [
        pltpu.make_async_copy(
            act.at[:, pl.ds(pl.multiple_of(q * 2048 + flip(h, half) * 1024, 1024), 1024)],
            DA.at[half, pl.ds(128, 128)],
            a_sem.at[half],
        )
        for half in range(2)
    ]
    small_loads = [
        pltpu.make_async_copy(w_any, wv, a_sem.at[2]),
        pltpu.make_async_copy(b_any, bv, a_sem.at[3]),
    ]
    for copy in small_loads + loads:
        copy.start()

    pl.semaphore_wait(barrier, len(peers))

    r_own = q * 4 + yh * 2 + h

    def piece(q_, h_):
        return w_any.at[:, pl.ds(pl.multiple_of((q_ * 2 + h_) * 1024, 1024), 1024)]

    p0 = []
    for i in range(1, 16):
        q_, yh_, h_ = group_peer(i)
        p0.append(
            remote(
                piece(q_, h_), rbuf.at[r_own], p0_s.at[i], p0_r.at[i],
                dev(q_, yh_, 2 * p + h_, z, c),
            )
        )
    for copy in p0:
        start(copy)
    own = pltpu.make_async_copy(piece(q, h), rbuf.at[r_own], own_sem)
    own.start()

    def place(at):
        near, pair, r = at >> 5, (at >> 4) & 1, at & 15
        far = (near + 1) >> 1
        z_ = z + jnp.where((near & 1) == 1, -far, far)
        z_ = jnp.where(z_ < 0, z_ + 12, jnp.where(z_ >= 12, z_ - 12, z_))
        x_ = 2 * (p + pair - 2 * p * pair) + (r & 1)
        return (r >> 2) * 96 + z_ * 8 + ((r >> 1) & 1) * 4 + x_

    col = lax.broadcasted_iota(jnp.int32, (96, 384), 1)
    row = lax.broadcasted_iota(jnp.int32, (96, 384), 0)
    hot[...] = jnp.where(place(col) == q * 96 + row, 1.0, 0.0).astype(bf16)
    held = place(lax.broadcasted_iota(jnp.int32, (384, 128), 0))
    for i in range(3):
        to = lax.broadcasted_iota(jnp.int32, (384, 128), 1) + i * 128
        turn[:, i * 128 : i * 128 + 128] = jnp.where(held == to, 1.0, 0.0).astype(bf16)
    for copy in small_loads:
        copy.wait()
    bias8 = jnp.broadcast_to(bv[...], (8, 96))
    bias_wide = sum(nn(part, hot[...]) for part in split3(bias8))[0:1, :]
    own.wait()
    for copy in p0:
        copy.wait_recv()
    W[0, 0, 0] = jnp.concatenate([rbuf[i] for i in range(16)], axis=0).astype(bf16)

    def az(t, dz, s):
        to = slot(dz - s) if dz - s != -6 else 11
        return remote(
            W.at[0, slot(dz), t], W.at[0, to, t], az_s.at[t, to], az_r.at[t, to], z_peer(s)
        )

    def wait_z(t, dz):
        b = W.at[0, slot(dz), t]
        remote(b, b, az_s.at[t, slot(dz)], az_r.at[t, slot(dz)], z_peer(1)).wait_recv()

    def ax(kind, dz):
        at = slot(dz)
        return remote(
            W.at[0, at, 0], W.at[1, at, KINDS[kind][1]], ax_s.at[kind, at], ax_r.at[kind, at],
            kind_peer(kind),
        )

    def along_x(dz):
        start(ax(1, dz))
        start(ax(2, dz))

    def wait_x(dz):
        ax(1, dz).wait_recv()
        ax(2, dz).wait_recv()

    STRIDE = (3, 2)

    def onward(t, dz):
        if dz % STRIDE[t]:
            return
        for way in ((1, -1) if dz == 0 else (1,) if dz < 0 else (-1,)):
            for hops in range(STRIDE[t], 0, -1):
                far = abs(dz) + hops
                if far > 6 or (far == 6 and (way == 1) == (t == 1)):
                    continue
                start(az(t, dz, way * hops))

    def pass_on(events):
        for t, dz in events:
            wait_z(t, dz)
            if dz != 6:
                onward(t, dz)
            if t == 0:
                along_x(dz)

    two = remote(W.at[0, 0, 0], W.at[0, 0, 1], ad_s, ad_r, kind_peer(0))
    start(two)
    onward(0, 0)
    along_x(0)
    two.wait_recv()
    onward(1, 0)
    pass_on(((0, -1), (0, 1), (0, -2), (0, 2), (0, -3), (0, 3), (1, -2), (1, 2), (0, -4), (0, 4), (0, -5), (0, 5), (0, 6), (1, -4), (1, 4)))
    for copy in loads:
        copy.wait()

    def rows(half, chunk):
        first, last = CHUNKS[chunk]
        return W[half, first:last].reshape(32 * (last - first), 1024)

    def lanes(chunk):
        first, last = CHUNKS[chunk]
        return slice(32 * first, 32 * last)

    pq, pr, C = (pqa, pqb), (pra, prb), (ca, cb)
    dq, dr, E = (dqa, dqb), (dra, drb), (ea, eb)

    def to_slabs(send, recv, chunk, s, r):
        copies = [
            remote(send.at[lax.rem(q + d, 4)], recv.at[d], s.at[chunk, d], r.at[chunk, d], q_peer(d))
            for d in (2, 1, 3)
        ]
        for copy in copies:
            start(copy)
        return copies

    def share(buffer, chunk, s, r):
        for d in (2, 1, 3):
            start(
                remote(buffer.at[q], buffer.at[q], s.at[chunk, d], r.at[chunk, d], q_peer(d))
            )

    def shared(buffer, chunk, s, r):
        for d in (1, 3, 2):
            b = buffer.at[lax.rem(q + 4 - d, 4)]
            remote(b, b, s.at[chunk, d], r.at[chunk, d], q_peer(d)).wait_recv()
        return buffer[...].reshape(128, buffer.shape[2])

    def make_pre(chunk):
        part = nt(DA[0, 128:256], rows(0, chunk)) + nt(DA[1, 128:256], rows(1, chunk))
        part = part + bias_wide[:, lanes(chunk)]
        pq[chunk][...] = part.reshape(4, 32, part.shape[1])
        return to_slabs(pq[chunk], pr[chunk], chunk, pre_s, pre_r)

    def make_codes(chunk, copies):
        for copy in copies:
            copy.wait_recv()
        s, r = pq[chunk], pr[chunk]
        pre = (s[q] + r[1]) + (r[2] + r[3])
        codes = jnp.maximum(pre, 0.0)
        C[chunk][q] = codes.astype(bf16)
        share(C[chunk], chunk, code_s, code_r)
        return pre, codes

    for dz in (0, -1, 1, -2, 2, -3, 3, -4):
        wait_x(dz)
    for dz in (-1, 1, -3, 3):
        wait_z(1, dz)
    copies_a = make_pre(0)
    pass_on(())
    for dz in (-5, 5, 6):
        wait_z(1, dz)
    for dz in (4, -5, 5, 6):
        wait_x(dz)
    copies_b = make_pre(1)
    pre_a, codes_a = make_codes(0, copies_a)

    ones = jnp.ones((8, 1024), bf16)
    for chunk in range(2):
        squares = None
        for half in range(2):
            wide = rows(half, chunk).astype(f32)
            sq = wide * wide
            hi = sq.astype(bf16)
            low = (sq - hi.astype(f32)).astype(bf16)
            part = nt(ones, hi) + nt(ones, low)
            squares = part if squares is None else squares + part
        for s in range(4):
            dq[chunk][s, 32:40] = squares

    pre_b, codes_b = make_codes(1, copies_b)
    low = [shared(C[chunk], chunk, code_s, code_r) for chunk in range(2)]

    core_send = []
    for half in range(2):
        part = nn(low[0], rows(half, 0)) + nn(low[1], rows(half, 1))
        rown[half] = part
        rs[half] = part.astype(bf16)
        copy = remote(rs.at[half], rr.at[half], core_s.at[half], core_r.at[half], core_peer)
        start(copy)
        core_send.append(copy)
    for chunk in range(2):
        LT[lanes(chunk), 0:128] = jnp.transpose(low[chunk].astype(f32)).astype(bf16)
    squared = jnp.zeros((1, 128), f32)
    for half in range(2):
        core_send[half].wait_recv()
        for t in range(4):
            at = slice(t * 32, t * 32 + 32)
            error = (rown[half, at] + rr[half, at].astype(f32)) - DA[
                half, 128 + t * 32 : 160 + t * 32
            ].astype(f32)
            DA[half, at] = (error * (2.0 / TOKENS)).astype(bf16)
            squared = squared + fold(jnp.sum(error * error, axis=0, keepdims=True))

    def make_dcode(chunk):
        part = nt(DA[0, 0:128], rows(0, chunk)) + nt(DA[1, 0:128], rows(1, chunk))
        for s in range(4):
            dq[chunk][s, 0:32] = part[s * 32 : s * 32 + 32]
        return to_slabs(dq[chunk], dr[chunk], chunk, dc_s, dc_r)

    def make_dpre(chunk, copies, pre):
        for copy in copies:
            copy.wait_recv()
        s, r = dq[chunk], dr[chunk]
        dcode = (s[q] + r[1]) + (r[2] + r[3])
        norms = jnp.sqrt(dcode[32:33] + 1e-6)
        dpre = jnp.where(pre > 0, dcode[0:32] + (sparsity / TOKENS) * norms, 0.0)
        E[chunk][q] = dpre.astype(bf16)
        share(E[chunk], chunk, dp_s, dp_r)
        return dpre, norms

    dcode_b = make_dcode(1)
    dcode_a = make_dcode(0)
    dpre_b, norms_b = make_dpre(1, dcode_b, pre_b)
    dpre_a, norms_a = make_dpre(0, dcode_a, pre_a)

    def make_grad(chunk):
        first, last = CHUNKS[chunk]
        dpre_low = shared(E[chunk], chunk, dp_s, dp_r)
        LT[lanes(chunk), 128:256] = jnp.transpose(dpre_low.astype(f32)).astype(bf16)
        for half in range(2):
            part = nn(LT[lanes(chunk)], DA[half])
            gs[half, first:last] = part.astype(bf16).reshape(last - first, 2, 16, 1024)

    def gx(at, kind):
        half, pair = KINDS[kind]
        return remote(
            gs.at[half, at, pair], gr.at[kind, at], gx_s.at[kind, at], gx_r.at[kind, at],
            kind_peer(kind),
        )

    make_grad(1)

    @pl.loop(0, 4)
    def _(i):
        for kind in range(3):
            gx(11 - i, kind).start()

    bias_part = jnp.concatenate(
        [jnp.sum(v, axis=0, keepdims=True) for v in (dpre_a, dpre_b)], axis=1
    )
    counts = jnp.concatenate(
        [jnp.sum(v, axis=0, keepdims=True) for v in (codes_a, codes_b)], axis=1
    )
    norms = jnp.concatenate([norms_a, norms_b], axis=1)
    loss_part = 0.5 * squared + sparsity * fold(counts * norms)
    both = jnp.concatenate([bias_part, counts, jnp.zeros((6, 384), f32)], axis=0)
    both = sum(nn(part, turn[...]) for part in split3(both))
    vx[x] = jnp.concatenate(
        [both[0:1, i * 128 : i * 128 + 128] for i in range(3)]
        + [both[1:2, i * 128 : i * 128 + 128] for i in range(3)]
        + [loss_part, jnp.zeros((1, 128), f32)],
        axis=0,
    )
    for d in range(1, 4):
        start(remote(vx.at[x], vx.at[x], vx_s.at[d], vx_r.at[d], x_peer(d)))

    make_grad(0)

    @pl.loop(4, 12)
    def _(i):
        for kind in range(3):
            gx(11 - i, kind).start()

    for done in started:
        done()
    started.clear()

    def x_sent():
        @pl.loop(0, 12)
        def _(i):
            for kind in range(3):
                gx(i, kind).wait_send()

    started.append(x_sent)

    for d in range(1, 4):
        b = vx.at[lax.rem(x + 4 - d, 4)]
        remote(b, b, vx_s.at[d], vx_r.at[d], x_peer(d)).wait_recv()
    y = yh * 4 + q
    vy[y] = (vx[0] + vx[1]) + (vx[2] + vx[3])
    for d in range(1, 8):
        start(remote(vy.at[y], vy.at[y], vy_s.at[d], vy_r.at[d], y_peer(d)))

    def reduce_x(at):
        for kind in (1, 2, 0):
            gx(at, kind).wait_recv()
        return (gs[0, at, 0].astype(f32) + gr[0, at].astype(f32)) + (
            gr[1, at].astype(f32) + gr[2, at].astype(f32)
        )

    def gz(at):
        far = lax.div(at + 1, 2)
        far = far - jnp.where(far > 3, 3, 0)
        sign = 1 - 2 * lax.rem(at, 2)
        sign = jnp.where(at == 11, 1, sign)
        return remote(hs.at[at], hr.at[at], gz_s.at[at], gz_r.at[at], z_peer(sign * far))

    def send_z(at, more=()):
        part = reduce_x(at)
        for other in more:
            gz(other).wait_recv()
            part = part + hr[other].astype(f32)
        hs[at] = part.astype(bf16)
        gz(at).start()

    @pl.loop(0, 5)
    def _(i):
        send_z(11 - i)

    for d in range(1, 8):
        b = vy.at[lax.rem(y + 8 - d, 8)]
        remote(b, b, vy_s.at[d], vy_r.at[d], y_peer(d)).wait_recv()
    v = vy[0]
    for i in range(1, 8):
        v = v + vy[i]
    vz[z] = v
    for d in range(1, 12):
        start(remote(vz.at[z], vz.at[z], vz_s.at[d], vz_r.at[d], z_peer(d)))

    send_z(6, (8, 10, 11))
    send_z(5, (7, 9))

    @pl.loop(7, 11)
    def _(i):
        send_z(11 - i)

    def z_sent():
        @pl.loop(1, 12)
        def _(k):
            gz(k).wait_send()

    started.append(z_sent)
    hown[...] = reduce_x(0)

    for d in range(1, 12):
        b = vz.at[lax.rem(z + 12 - d, 12)]
        remote(b, b, vz_s.at[d], vz_r.at[d], z_peer(d)).wait_recv()
    v = vz[0]
    for i in range(1, 12):
        v = v + vz[i]
    vc[0] = v
    vc_send = remote(vc.at[0], vc.at[1], vc_s.at[0], vc_r.at[0], core_peer)
    start(vc_send)

    @pl.loop(0, 6)
    def _(i):
        gz(6 - i).wait_recv()
        hown[...] += hr[6 - i].astype(f32)

    total = hown[...]
    for i in range(16):
        fs[i] = total[i : i + 1]
    mine = (q * 2 + h) * 2 + yh
    fin = []
    for i in range(1, 16):
        q_, yh_, h_ = group_peer(i)
        fin.append(
            remote(
                fs.at[q_ * 4 + yh_ * 2 + h_], fr.at[mine], fin_s.at[i], fin_r.at[i],
                dev(q_, yh_, 2 * p + h_, z, c),
            )
        )
    for copy in fin:
        start(copy)
    fr[mine] = fs[r_own]

    bias8 = jnp.concatenate([v[0:1], v[1:2], v[2:3]], axis=1)
    bias8 = jnp.broadcast_to(bias8, (8, 384))
    pick = jnp.where(col == q * 96 + row, 1.0, 0.0).astype(bf16)
    bias_grad = sum(nt(part, pick) for part in split3(bias8))[0:1, :]
    lane = lax.broadcasted_iota(jnp.int32, (1, 128), 1)
    own_count = jnp.zeros((1, 128), f32)
    for i in range(3):
        own_count = own_count + jnp.where(lane + i * 128 == q * 96 + g, v[3 + i : 4 + i], 0.0)
    own_count = jnp.sum(own_count, axis=1, keepdims=True)
    vc_send.wait_recv()
    loss = jnp.sum(v[6:7] + vc[1, 6:7], axis=1, keepdims=True) * (1.0 / TOKENS)
    small_ref[...] = jnp.zeros((8, 128), f32)
    small_ref[0:1, 0:96] = bias_grad
    small_ref[1:2, :] = jnp.broadcast_to(loss, (1, 128))

    for done in started[:-15]:
        done()
    own_row = wv[...].astype(bf16).astype(f32)
    own_norm = jnp.sqrt(jnp.sum(own_row * own_row, axis=1, keepdims=True) + 1e-6)
    scale = (sparsity / TOKENS) * own_count / own_norm
    for copy in fin:
        copy.wait_recv()
    for s in range(8):
        at = slice(s * 1024, s * 1024 + 1024)
        grad_ref[:, at] = (fr[2 * s] + fr[2 * s + 1]) + scale * own_row[:, at]

    for done in started[-15:]:
        done()


def step(activations, weight, code_bias):
    dma = pltpu.SemaphoreType.DMA
    vmem = pltpu.VMEM
    return pl.pallas_call(
        kernel,
        out_shape=(
            jax.ShapeDtypeStruct((1, 8192), f32),
            jax.ShapeDtypeStruct((8, 128), f32),
        ),
        in_specs=[pl.BlockSpec(memory_space=pl.ANY)] * 3,
        out_specs=[pl.BlockSpec(memory_space=pltpu.VMEM)] * 2,
        scratch_shapes=[
            vmem((1, 8192), f32),
            vmem((1, 96), f32),
            vmem((16, 1, 1024), f32),
            vmem((2, 12, 2, 16, 1024), bf16),
            vmem((2, 256, 1024), bf16),
            vmem((384, 256), bf16),
            vmem((4, 32, 256), f32), vmem((4, 32, 128), f32),
            vmem((4, 32, 256), f32), vmem((4, 32, 128), f32),
            vmem((4, 32, 256), bf16), vmem((4, 32, 128), bf16),
            vmem((2, 128, 1024), f32),
            vmem((2, 128, 1024), bf16),
            vmem((2, 128, 1024), bf16),
            vmem((4, 40, 256), f32), vmem((4, 40, 128), f32),
            vmem((4, 40, 256), f32), vmem((4, 40, 128), f32),
            vmem((4, 32, 256), bf16), vmem((4, 32, 128), bf16),
            vmem((2, 12, 2, 16, 1024), bf16),
            vmem((3, 12, 16, 1024), bf16),
            vmem((12, 16, 1024), bf16),
            vmem((12, 16, 1024), bf16),
            vmem((16, 1024), f32),
            vmem((16, 1, 1024), f32),
            vmem((16, 1, 1024), f32),
            vmem((4, 8, 128), f32),
            vmem((8, 8, 128), f32),
            vmem((12, 8, 128), f32),
            vmem((2, 8, 128), f32),
            vmem((96, 384), bf16),
            vmem((384, 384), bf16),
            dma((4,)),
            dma,
            dma((16,)), dma((16,)),
            dma((3, 12)), dma((3, 12)),
            dma, dma,
            dma((2, 12)), dma((2, 12)),
            dma((2, 4)), dma((2, 4)),
            dma((2, 4)), dma((2, 4)),
            dma((2,)), dma((2,)),
            dma((2, 4)), dma((2, 4)),
            dma((2, 4)), dma((2, 4)),
            dma((3, 12)), dma((3, 12)),
            dma((12,)), dma((12,)),
            dma((16,)), dma((16,)),
            dma((4,)), dma((4,)),
            dma((8,)), dma((8,)),
            dma((12,)), dma((12,)),
            dma((1,)), dma((1,)),
        ],
        compiler_params=pltpu.CompilerParams(
            collective_id=0, has_side_effects=True, vmem_limit_bytes=52 * 1024 * 1024
        ),
    )(activations, weight, code_bias.reshape(1, 96))


def per_device(activations, weight, weight_mean, weight_square, code_bias, bias_mean, bias_square):
    grad_own, small = step(activations, weight, code_bias)
    bias_grad = small[0, :96]
    total_loss = small[1, 0]
    after_weight, after_mean, after_square = adam_step(weight, weight_mean, weight_square, grad_own)
    after_bias, after_biasmean, after_biassquare = adam_step(
        code_bias, bias_mean, bias_square, bias_grad
    )
    return (
        after_weight,
        after_mean,
        after_square,
        after_bias,
        after_biasmean,
        after_biassquare,
        total_loss,
    )


def solution(mesh):
    placed = (
        P("dp", None),
        P(("latent", "dp"), None),
        P(("latent", "dp"), None),
        P(("latent", "dp"), None),
        P("latent"),
        P("latent"),
        P("latent"),
    )
    return jax.shard_map(
        per_device,
        mesh=mesh,
        in_specs=placed,
        out_specs=(
            P(("latent", "dp"), None),
            P(("latent", "dp"), None),
            P(("latent", "dp"), None),
            P("latent"),
            P("latent"),
            P("latent"),
            P(),
        ),
        check_vma=False,
    )
```

```python
import functools

import jax
import jax.numpy as jnp
from jax import lax
from jax.experimental import pallas as pl
from jax.experimental.pallas import tpu as pltpu
from jax.sharding import PartitionSpec as P

sparsity = 2.0
first_decay = 0.9
second_decay = 0.999
learn_rate = 0.002
adam_floor = 1e-08
first_fix = 0.9999734386011124
second_fix = 0.09520785288629108

TOKENS = 12288
MESH = pl.DeviceIdType.MESH
bf16 = jnp.bfloat16
f32 = jnp.float32


def adam_step(value, mean, square, grad):
    mean_new = first_decay * mean + (1.0 - first_decay) * grad
    square_new = second_decay * square + (1.0 - second_decay) * grad * grad
    value_new = value - learn_rate * (mean_new / first_fix) / (
        jnp.sqrt(square_new / second_fix) + adam_floor
    )
    return (value_new, mean_new, square_new)


def split3(v):
    hi = v.astype(bf16)
    rest = v - hi.astype(f32)
    mid = rest.astype(bf16)
    low = (rest - mid.astype(f32)).astype(bf16)
    return hi, mid, low


def nt(a, b):
    return lax.dot_general(a, b, (((1,), (1,)), ((), ())), preferred_element_type=f32)


def nn(a, b):
    return jnp.dot(a, b, preferred_element_type=f32)


def fold(v):
    total = v[:, 0:128]
    for i in range(1, v.shape[1] // 128):
        total = total + v[:, i * 128 : (i + 1) * 128]
    return total


def slot(dz):
    if dz == 6:
        return 11
    return -2 * dz - 1 if dz < 0 else 2 * dz


KINDS = ((0, 1), (1, 1), (1, 0))
CHUNKS = ((0, 8), (8, 12))
FIRST = (3, 11, 7, 15, 2, 10, 6, 14, 9, 5, 13, 8, 4, 12, 1)


def kernel(
    act, w_any, b_any, grad_ref, small_ref,
    wv, bv, rbuf, W, DA, LT, pqa, pqb, pra, prb, ca, cb, rown, rs, rr,
    dqa, dqb, dra, drb, ea, eb, gs, gr, hs, hr, hown, fs, fr,
    vx, vy, vz, vc, hot, turn,
    a_sem, own_sem,
    p0_s, p0_r, ax_s, ax_r, ad_s, ad_r, az_s, az_r,
    pre_s, pre_r, code_s, code_r, core_s, core_r, dc_s, dc_r, dp_s, dp_r,
    gx_s, gx_r, gz_s, gz_r, fin_s, fin_r, vx_s, vx_r, vy_s, vy_r, vz_s, vz_r, vc_s, vc_r,
):
    l = lax.axis_index("latent")
    g = lax.axis_index("dp")
    q, c = lax.div(l, 2), lax.rem(l, 2)
    x, yh, z = lax.rem(g, 4), lax.rem(lax.div(g, 4), 2), lax.div(g, 8)
    p, h = lax.div(x, 2), lax.rem(x, 2)

    def dev(q_, yh_, x_, z_, c_):
        return (q_ * 2 + c_, z_ * 8 + yh_ * 4 + x_)

    def group_peer(i):
        q_ = lax.rem(q + (i // 4), 4)
        yh_ = lax.rem(yh + (i // 2) % 2, 2)
        h_ = lax.rem(h + i % 2, 2)
        return q_, yh_, h_

    def flip(bit, by):
        return 1 - bit if by else bit

    def kind_peer(kind):
        half, pair = KINDS[kind]
        return dev(q, yh, 2 * flip(p, pair) + flip(h, half), z, c)

    def x_peer(d):
        return dev(q, yh, lax.rem(x + d, 4), z, c)

    def q_peer(d):
        return dev(lax.rem(q + d, 4), yh, x, z, c)

    def z_peer(d):
        return dev(q, yh, x, lax.rem(z + d + 12, 12), c)

    def y_peer(d):
        y_ = lax.rem(yh * 4 + q + d, 8)
        return dev(lax.rem(y_, 4), lax.div(y_, 4), x, z, c)

    core_peer = dev(q, yh, x, z, 1 - c)
    started = []

    def remote(src, dst, s, r, to):
        return pltpu.make_async_remote_copy(
            src_ref=src, dst_ref=dst, send_sem=s, recv_sem=r, device_id=to, device_id_type=MESH
        )

    def start(copy):
        copy.start()
        started.append(copy.wait_send)

    barrier = pltpu.get_barrier_semaphore()
    peers = []
    for i in FIRST:
        q_, yh_, h_ = group_peer(i)
        peers.append(dev(q_, yh_, 2 * p + h_, z, c))
    peers += [kind_peer(0), kind_peer(1)] + [z_peer(d) for d in range(1, 12)] + [core_peer]
    for peer in peers:
        pl.semaphore_signal(barrier, inc=1, device_id=peer, device_id_type=MESH)

    loads = [
        pltpu.make_async_copy(
            act.at[:, pl.ds(pl.multiple_of(q * 2048 + flip(h, half) * 1024, 1024), 1024)],
            DA.at[half, pl.ds(128, 128)],
            a_sem.at[half],
        )
        for half in range(2)
    ]
    small_loads = [
        pltpu.make_async_copy(w_any, wv, a_sem.at[2]),
        pltpu.make_async_copy(b_any, bv, a_sem.at[3]),
    ]
    for copy in small_loads + loads:
        copy.start()

    pl.semaphore_wait(barrier, len(peers))

    r_own = q * 4 + yh * 2 + h

    def piece(q_, h_):
        return w_any.at[:, pl.ds(pl.multiple_of((q_ * 2 + h_) * 1024, 1024), 1024)]

    p0 = []
    for i in FIRST:
        q_, yh_, h_ = group_peer(i)
        p0.append(
            remote(
                piece(q_, h_), rbuf.at[r_own], p0_s.at[i], p0_r.at[i],
                dev(q_, yh_, 2 * p + h_, z, c),
            )
        )
    for copy in p0:
        start(copy)
    own = pltpu.make_async_copy(piece(q, h), rbuf.at[r_own], own_sem)
    own.start()

    def place(at):
        near, pair, r = at >> 5, (at >> 4) & 1, at & 15
        far = (near + 1) >> 1
        z_ = z + jnp.where((near & 1) == 1, -far, far)
        z_ = jnp.where(z_ < 0, z_ + 12, jnp.where(z_ >= 12, z_ - 12, z_))
        x_ = 2 * (p + pair - 2 * p * pair) + (r & 1)
        return (r >> 2) * 96 + z_ * 8 + ((r >> 1) & 1) * 4 + x_

    col = lax.broadcasted_iota(jnp.int32, (96, 384), 1)
    row = lax.broadcasted_iota(jnp.int32, (96, 384), 0)
    hot[...] = jnp.where(place(col) == q * 96 + row, 1.0, 0.0).astype(bf16)
    held = place(lax.broadcasted_iota(jnp.int32, (384, 128), 0))
    for i in range(3):
        to = lax.broadcasted_iota(jnp.int32, (384, 128), 1) + i * 128
        turn[:, i * 128 : i * 128 + 128] = jnp.where(held == to, 1.0, 0.0).astype(bf16)
    for copy in small_loads:
        copy.wait()
    bias8 = jnp.broadcast_to(bv[...], (8, 96))
    bias_wide = sum(nn(part, hot[...]) for part in split3(bias8))[0:1, :]
    own.wait()
    for copy in p0:
        copy.wait_recv()
    W[0, 0, 0] = jnp.concatenate([rbuf[i] for i in range(16)], axis=0).astype(bf16)

    def az(t, dz, s):
        to = slot(dz - s) if dz - s != -6 else 11
        return remote(
            W.at[0, slot(dz), t], W.at[0, to, t], az_s.at[t, to], az_r.at[t, to], z_peer(s)
        )

    def wait_z(t, dz):
        b = W.at[0, slot(dz), t]
        remote(b, b, az_s.at[t, slot(dz)], az_r.at[t, slot(dz)], z_peer(1)).wait_recv()

    def ax(kind, dz):
        at = slot(dz)
        half, pair = KINDS[kind]
        return remote(
            W.at[0, at, 0], W.at[half, at, pair], ax_s.at[kind, at], ax_r.at[kind, at],
            kind_peer(kind),
        )

    FAR = (-5, 5, 6)

    def along_x(dz):
        if dz in FAR:
            start(ax(0, dz))
        start(ax(1, dz))
        start(ax(2, dz))

    def wait_x(dz):
        ax(1, dz).wait_recv()
        ax(2, dz).wait_recv()

    STRIDE = (3, 2)

    def onward(t, dz):
        if dz % STRIDE[t]:
            return
        for way in ((1, -1) if dz == 0 else (1,) if dz < 0 else (-1,)):
            for hops in range(STRIDE[t], 0, -1):
                far = abs(dz) + hops
                if far > (6, 4)[t] or (far == 6 and way == -1):
                    continue
                start(az(t, dz, way * hops))

    def pass_on(events):
        for t, dz in events:
            wait_z(t, dz)
            if dz != 6:
                onward(t, dz)
            if t == 0:
                along_x(dz)

    two = remote(W.at[0, 0, 0], W.at[0, 0, 1], ad_s, ad_r, kind_peer(0))
    start(two)
    onward(0, 0)
    along_x(0)
    two.wait_recv()
    onward(1, 0)
    pass_on(((0, -1), (0, 1), (0, -2), (0, 2), (0, -3), (0, 3), (1, -2), (1, 2), (0, -4), (0, 4), (0, -5), (0, 5), (0, 6)))
    for copy in loads:
        copy.wait()

    def rows(half, chunk):
        first, last = CHUNKS[chunk]
        return W[half, first:last].reshape(32 * (last - first), 1024)

    def lanes(chunk):
        first, last = CHUNKS[chunk]
        return slice(32 * first, 32 * last)

    pq, pr, C = (pqa, pqb), (pra, prb), (ca, cb)
    dq, dr, E = (dqa, dqb), (dra, drb), (ea, eb)

    def to_slabs(send, recv, chunk, s, r):
        copies = [
            remote(send.at[lax.rem(q + d, 4)], recv.at[d], s.at[chunk, d], r.at[chunk, d], q_peer(d))
            for d in (2, 1, 3)
        ]
        for copy in copies:
            start(copy)
        return copies

    def share(buffer, chunk, s, r):
        for d in (2, 1, 3):
            start(
                remote(buffer.at[q], buffer.at[q], s.at[chunk, d], r.at[chunk, d], q_peer(d))
            )

    def shared(buffer, chunk, s, r):
        for d in (1, 3, 2):
            b = buffer.at[lax.rem(q + 4 - d, 4)]
            remote(b, b, s.at[chunk, d], r.at[chunk, d], q_peer(d)).wait_recv()
        return buffer[...].reshape(128, buffer.shape[2])

    def make_pre(chunk):
        part = nt(DA[0, 128:256], rows(0, chunk)) + nt(DA[1, 128:256], rows(1, chunk))
        part = part + bias_wide[:, lanes(chunk)]
        pq[chunk][...] = part.reshape(4, 32, part.shape[1])
        return to_slabs(pq[chunk], pr[chunk], chunk, pre_s, pre_r)

    def make_codes(chunk, copies):
        for copy in copies:
            copy.wait_recv()
        s, r = pq[chunk], pr[chunk]
        pre = (s[q] + r[1]) + (r[2] + r[3])
        codes = jnp.maximum(pre, 0.0)
        C[chunk][q] = codes.astype(bf16)
        share(C[chunk], chunk, code_s, code_r)
        return pre, codes

    for dz in (0, -1, 1, -2, 2, -3, 3, -4):
        wait_x(dz)
    for dz in (-1, 1, -3, 3, -4):
        wait_z(1, dz)
    copies_a = make_pre(0)
    wait_z(1, 4)
    for dz in FAR:
        ax(0, dz).wait_recv()
    for dz in (4, -5, 5, 6):
        wait_x(dz)
    copies_b = make_pre(1)
    pre_a, codes_a = make_codes(0, copies_a)

    ones = jnp.ones((8, 1024), bf16)
    for chunk in range(2):
        squares = None
        for half in range(2):
            wide = rows(half, chunk).astype(f32)
            sq = wide * wide
            hi = sq.astype(bf16)
            low = (sq - hi.astype(f32)).astype(bf16)
            part = nt(ones, hi) + nt(ones, low)
            squares = part if squares is None else squares + part
        for s in range(4):
            dq[chunk][s, 32:40] = squares

    pre_b, codes_b = make_codes(1, copies_b)
    low = [shared(C[chunk], chunk, code_s, code_r) for chunk in range(2)]

    core_send = []
    for half in range(2):
        for part_at in range(2):
            cols = slice(part_at * 512, part_at * 512 + 512)
            part = nn(low[0], W[half, 0:8, :, :, cols].reshape(256, 512)) + nn(
                low[1], W[half, 8:12, :, :, cols].reshape(128, 512)
            )
            rown[half, :, cols] = part
            rs[half, :, cols] = part.astype(bf16)
            i = 2 * half + part_at
            lane = pl.ds(part_at * 512, 512)
            copy = remote(
                rs.at[half, :, lane], rr.at[half, :, lane], core_s.at[i], core_r.at[i], core_peer
            )
            start(copy)
            core_send.append(copy)
    for chunk in range(2):
        LT[lanes(chunk), 0:128] = jnp.transpose(low[chunk].astype(f32)).astype(bf16)
    squared = jnp.zeros((1, 128), f32)
    for half in range(2):
        for part_at in range(2):
            cols = slice(part_at * 512, part_at * 512 + 512)
            core_send[2 * half + part_at].wait_recv()
            for t in range(4):
                at = slice(t * 32, t * 32 + 32)
                error = (rown[half, at, cols] + rr[half, at, cols].astype(f32)) - DA[
                    half, 128 + t * 32 : 160 + t * 32, cols
                ].astype(f32)
                DA[half, at, cols] = (error * (2.0 / TOKENS)).astype(bf16)
                squared = squared + fold(jnp.sum(error * error, axis=0, keepdims=True))

    def make_dcode(chunk):
        part = nt(DA[0, 0:128], rows(0, chunk)) + nt(DA[1, 0:128], rows(1, chunk))
        for s in range(4):
            dq[chunk][s, 0:32] = part[s * 32 : s * 32 + 32]
        return to_slabs(dq[chunk], dr[chunk], chunk, dc_s, dc_r)

    def make_dpre(chunk, copies, pre):
        for copy in copies:
            copy.wait_recv()
        s, r = dq[chunk], dr[chunk]
        dcode = (s[q] + r[1]) + (r[2] + r[3])
        norms = jnp.sqrt(dcode[32:33] + 1e-6)
        dpre = jnp.where(pre > 0, dcode[0:32] + (sparsity / TOKENS) * norms, 0.0)
        E[chunk][q] = dpre.astype(bf16)
        share(E[chunk], chunk, dp_s, dp_r)
        return dpre, norms

    dcode_b = make_dcode(1)
    dcode_a = make_dcode(0)
    dpre_b, norms_b = make_dpre(1, dcode_b, pre_b)
    dpre_a, norms_a = make_dpre(0, dcode_a, pre_a)

    def make_grad(chunk):
        first, last = CHUNKS[chunk]
        dpre_low = shared(E[chunk], chunk, dp_s, dp_r)
        LT[lanes(chunk), 128:256] = jnp.transpose(dpre_low.astype(f32)).astype(bf16)
        for half in range(2):
            part = nn(LT[lanes(chunk)], DA[half])
            gs[half, first:last] = part.astype(bf16).reshape(last - first, 2, 16, 1024)

    def gx(at, kind):
        half, pair = KINDS[kind]
        return remote(
            gs.at[half, at, pair], gr.at[kind, at], gx_s.at[kind, at], gx_r.at[kind, at],
            kind_peer(kind),
        )

    make_grad(1)

    @pl.loop(0, 4)
    def _(i):
        for kind in range(3):
            gx(11 - i, kind).start()

    bias_part = jnp.concatenate(
        [jnp.sum(v, axis=0, keepdims=True) for v in (dpre_a, dpre_b)], axis=1
    )
    counts = jnp.concatenate(
        [jnp.sum(v, axis=0, keepdims=True) for v in (codes_a, codes_b)], axis=1
    )
    norms = jnp.concatenate([norms_a, norms_b], axis=1)
    loss_part = 0.5 * squared + sparsity * fold(counts * norms)
    both = jnp.concatenate([bias_part, counts, jnp.zeros((6, 384), f32)], axis=0)
    both = sum(nn(part, turn[...]) for part in split3(both))
    y = yh * 4 + q
    vy[y] = jnp.concatenate(
        [both[0:1, i * 128 : i * 128 + 128] for i in range(3)]
        + [both[1:2, i * 128 : i * 128 + 128] for i in range(3)]
        + [loss_part, jnp.zeros((1, 128), f32)],
        axis=0,
    )
    for d in range(1, 8):
        start(remote(vy.at[y], vy.at[y], vy_s.at[d], vy_r.at[d], y_peer(d)))

    make_grad(0)

    @pl.loop(4, 12)
    def _(i):
        for kind in range(3):
            gx(11 - i, kind).start()

    for done in started:
        done()
    started.clear()

    def x_sent():
        @pl.loop(0, 12)
        def _(i):
            for kind in range(3):
                gx(i, kind).wait_send()

    started.append(x_sent)

    for d in range(1, 8):
        b = vy.at[lax.rem(y + 8 - d, 8)]
        remote(b, b, vy_s.at[d], vy_r.at[d], y_peer(d)).wait_recv()
    v = vy[0]
    for i in range(1, 8):
        v = v + vy[i]
    vz[z] = v
    for d in range(1, 12):
        start(remote(vz.at[z], vz.at[z], vz_s.at[d], vz_r.at[d], z_peer(d)))

    def reduce_x(at):
        for kind in (1, 2, 0):
            gx(at, kind).wait_recv()
        return (gs[0, at, 0].astype(f32) + gr[0, at].astype(f32)) + (
            gr[1, at].astype(f32) + gr[2, at].astype(f32)
        )

    def gz(at):
        far = lax.div(at + 1, 2)
        far = far - jnp.where(far > 3, 3, 0)
        sign = 1 - 2 * lax.rem(at, 2)
        sign = jnp.where(at == 11, 1, sign)
        return remote(hs.at[at], hr.at[at], gz_s.at[at], gz_r.at[at], z_peer(sign * far))

    def send_z(at, more=()):
        part = reduce_x(at)
        for other in more:
            gz(other).wait_recv()
            part = part + hr[other].astype(f32)
        hs[at] = part.astype(bf16)
        gz(at).start()

    @pl.loop(0, 5)
    def _(i):
        send_z(11 - i)

    for d in range(1, 12):
        b = vz.at[lax.rem(z + 12 - d, 12)]
        remote(b, b, vz_s.at[d], vz_r.at[d], z_peer(d)).wait_recv()
    v = vz[0]
    for i in range(1, 12):
        v = v + vz[i]
    vx[x] = v
    for d in range(1, 4):
        start(remote(vx.at[x], vx.at[x], vx_s.at[d], vx_r.at[d], x_peer(d)))

    send_z(6, (8, 10, 11))
    send_z(5, (7, 9))

    @pl.loop(7, 11)
    def _(i):
        send_z(11 - i)

    def z_sent():
        @pl.loop(1, 12)
        def _(k):
            gz(k).wait_send()

    started.append(z_sent)
    hown[...] = reduce_x(0)

    for d in range(1, 4):
        b = vx.at[lax.rem(x + 4 - d, 4)]
        remote(b, b, vx_s.at[d], vx_r.at[d], x_peer(d)).wait_recv()
    v = (vx[0] + vx[1]) + (vx[2] + vx[3])
    vc[0] = v
    vc_send = remote(vc.at[0], vc.at[1], vc_s.at[0], vc_r.at[0], core_peer)
    start(vc_send)

    @pl.loop(0, 6)
    def _(i):
        gz(6 - i).wait_recv()
        hown[...] += hr[6 - i].astype(f32)

    total = hown[...]
    for i in range(16):
        fs[i] = total[i : i + 1]
    mine = (q * 2 + h) * 2 + yh
    fin = []
    for i in FIRST:
        q_, yh_, h_ = group_peer(i)
        fin.append(
            remote(
                fs.at[q_ * 4 + yh_ * 2 + h_], fr.at[mine], fin_s.at[i], fin_r.at[i],
                dev(q_, yh_, 2 * p + h_, z, c),
            )
        )
    for copy in fin:
        start(copy)
    fr[mine] = fs[r_own]

    bias8 = jnp.concatenate([v[0:1], v[1:2], v[2:3]], axis=1)
    bias8 = jnp.broadcast_to(bias8, (8, 384))
    pick = jnp.where(col == q * 96 + row, 1.0, 0.0).astype(bf16)
    bias_grad = sum(nt(part, pick) for part in split3(bias8))[0:1, :]
    lane = lax.broadcasted_iota(jnp.int32, (1, 128), 1)
    own_count = jnp.zeros((1, 128), f32)
    for i in range(3):
        own_count = own_count + jnp.where(lane + i * 128 == q * 96 + g, v[3 + i : 4 + i], 0.0)
    own_count = jnp.sum(own_count, axis=1, keepdims=True)
    vc_send.wait_recv()
    loss = jnp.sum(v[6:7] + vc[1, 6:7], axis=1, keepdims=True) * (1.0 / TOKENS)
    small_ref[...] = jnp.zeros((8, 128), f32)
    small_ref[0:1, 0:96] = bias_grad
    small_ref[1:2, :] = jnp.broadcast_to(loss, (1, 128))

    for done in started[:-15]:
        done()
    own_row = wv[...].astype(bf16).astype(f32)
    own_norm = jnp.sqrt(jnp.sum(own_row * own_row, axis=1, keepdims=True) + 1e-6)
    scale = (sparsity / TOKENS) * own_count / own_norm
    for copy in fin:
        copy.wait_recv()
    for s in range(8):
        at = slice(s * 1024, s * 1024 + 1024)
        grad_ref[:, at] = (fr[2 * s] + fr[2 * s + 1]) + scale * own_row[:, at]

    for done in started[-15:]:
        done()


def step(activations, weight, code_bias):
    dma = pltpu.SemaphoreType.DMA
    vmem = pltpu.VMEM
    return pl.pallas_call(
        kernel,
        out_shape=(
            jax.ShapeDtypeStruct((1, 8192), f32),
            jax.ShapeDtypeStruct((8, 128), f32),
        ),
        in_specs=[pl.BlockSpec(memory_space=pl.ANY)] * 3,
        out_specs=[pl.BlockSpec(memory_space=pltpu.VMEM)] * 2,
        scratch_shapes=[
            vmem((1, 8192), f32),
            vmem((1, 96), f32),
            vmem((16, 1, 1024), f32),
            vmem((2, 12, 2, 16, 1024), bf16),
            vmem((2, 256, 1024), bf16),
            vmem((384, 256), bf16),
            vmem((4, 32, 256), f32), vmem((4, 32, 128), f32),
            vmem((4, 32, 256), f32), vmem((4, 32, 128), f32),
            vmem((4, 32, 256), bf16), vmem((4, 32, 128), bf16),
            vmem((2, 128, 1024), f32),
            vmem((2, 128, 1024), bf16),
            vmem((2, 128, 1024), bf16),
            vmem((4, 40, 256), f32), vmem((4, 40, 128), f32),
            vmem((4, 40, 256), f32), vmem((4, 40, 128), f32),
            vmem((4, 32, 256), bf16), vmem((4, 32, 128), bf16),
            vmem((2, 12, 2, 16, 1024), bf16),
            vmem((3, 12, 16, 1024), bf16),
            vmem((12, 16, 1024), bf16),
            vmem((12, 16, 1024), bf16),
            vmem((16, 1024), f32),
            vmem((16, 1, 1024), f32),
            vmem((16, 1, 1024), f32),
            vmem((4, 8, 128), f32),
            vmem((8, 8, 128), f32),
            vmem((12, 8, 128), f32),
            vmem((2, 8, 128), f32),
            vmem((96, 384), bf16),
            vmem((384, 384), bf16),
            dma((4,)),
            dma,
            dma((16,)), dma((16,)),
            dma((3, 12)), dma((3, 12)),
            dma, dma,
            dma((2, 12)), dma((2, 12)),
            dma((2, 4)), dma((2, 4)),
            dma((2, 4)), dma((2, 4)),
            dma((4,)), dma((4,)),
            dma((2, 4)), dma((2, 4)),
            dma((2, 4)), dma((2, 4)),
            dma((3, 12)), dma((3, 12)),
            dma((12,)), dma((12,)),
            dma((16,)), dma((16,)),
            dma((4,)), dma((4,)),
            dma((8,)), dma((8,)),
            dma((12,)), dma((12,)),
            dma((1,)), dma((1,)),
        ],
        compiler_params=pltpu.CompilerParams(
            collective_id=0, has_side_effects=True, vmem_limit_bytes=52 * 1024 * 1024
        ),
    )(activations, weight, code_bias.reshape(1, 96))


def per_device(activations, weight, weight_mean, weight_square, code_bias, bias_mean, bias_square):
    grad_own, small = step(activations, weight, code_bias)
    bias_grad = small[0, :96]
    total_loss = small[1, 0]
    after_weight, after_mean, after_square = adam_step(weight, weight_mean, weight_square, grad_own)
    after_bias, after_biasmean, after_biassquare = adam_step(
        code_bias, bias_mean, bias_square, bias_grad
    )
    return (
        after_weight,
        after_mean,
        after_square,
        after_bias,
        after_biasmean,
        after_biassquare,
        total_loss,
    )


def solution(mesh):
    placed = (
        P("dp", None),
        P(("latent", "dp"), None),
        P(("latent", "dp"), None),
        P(("latent", "dp"), None),
        P("latent"),
        P("latent"),
        P("latent"),
    )
    return jax.shard_map(
        per_device,
        mesh=mesh,
        in_specs=placed,
        out_specs=(
            P(("latent", "dp"), None),
            P(("latent", "dp"), None),
            P(("latent", "dp"), None),
            P("latent"),
            P("latent"),
            P("latent"),
            P(),
        ),
        check_vma=False,
    )
```

```python
import functools

import jax
import jax.numpy as jnp
from jax import lax
from jax.experimental import pallas as pl
from jax.experimental.pallas import tpu as pltpu
from jax.sharding import PartitionSpec as P

sparsity = 2.0
first_decay = 0.9
second_decay = 0.999
learn_rate = 0.002
adam_floor = 1e-08
first_fix = 0.9999734386011124
second_fix = 0.09520785288629108

TOKENS = 12288
MESH = pl.DeviceIdType.MESH
bf16 = jnp.bfloat16
f32 = jnp.float32


def adam_step(value, mean, square, grad):
    mean_new = first_decay * mean + (1.0 - first_decay) * grad
    square_new = second_decay * square + (1.0 - second_decay) * grad * grad
    value_new = value - learn_rate * (mean_new / first_fix) / (
        jnp.sqrt(square_new / second_fix) + adam_floor
    )
    return (value_new, mean_new, square_new)


def split3(v):
    hi = v.astype(bf16)
    rest = v - hi.astype(f32)
    mid = rest.astype(bf16)
    low = (rest - mid.astype(f32)).astype(bf16)
    return hi, mid, low


def nt(a, b):
    return lax.dot_general(a, b, (((1,), (1,)), ((), ())), preferred_element_type=f32)


def nn(a, b):
    return jnp.dot(a, b, preferred_element_type=f32)


def fold(v):
    total = v[:, 0:128]
    for i in range(1, v.shape[1] // 128):
        total = total + v[:, i * 128 : (i + 1) * 128]
    return total


def slot(dz):
    if dz == 6:
        return 11
    return -2 * dz - 1 if dz < 0 else 2 * dz


KINDS = ((0, 1), (1, 1), (1, 0))
CHUNKS = ((0, 8), (8, 12))
FIRST = (3, 11, 7, 15, 2, 10, 6, 14, 9, 5, 13, 8, 4, 12, 1)


def kernel(
    act, w_any, b_any, grad_ref, small_ref,
    wv, bv, rbuf, W, DA, LT, pqa, pqb, pra, prb, ca, cb, rown, rs, rr,
    dqa, dqb, dra, drb, nrm, ea, eb, gs, gr, hs, hr, hown, fs, fr,
    vx, vy, vz, vc, hot, turn,
    a_sem, own_sem,
    p0_s, p0_r, ax_s, ax_r, ad_s, ad_r, az_s, az_r,
    pre_s, pre_r, code_s, code_r, core_s, core_r, dc_s, dc_r, nm_s, nm_r, dp_s, dp_r,
    gx_s, gx_r, gz_s, gz_r, fin_s, fin_r, vx_s, vx_r, vy_s, vy_r, vz_s, vz_r, vc_s, vc_r,
):
    l = lax.axis_index("latent")
    g = lax.axis_index("dp")
    q, c = lax.div(l, 2), lax.rem(l, 2)
    x, yh, z = lax.rem(g, 4), lax.rem(lax.div(g, 4), 2), lax.div(g, 8)
    p, h = lax.div(x, 2), lax.rem(x, 2)

    def dev(q_, yh_, x_, z_, c_):
        return (q_ * 2 + c_, z_ * 8 + yh_ * 4 + x_)

    def group_peer(i):
        q_ = lax.rem(q + (i // 4), 4)
        yh_ = lax.rem(yh + (i // 2) % 2, 2)
        h_ = lax.rem(h + i % 2, 2)
        return q_, yh_, h_

    def flip(bit, by):
        return 1 - bit if by else bit

    def kind_peer(kind):
        half, pair = KINDS[kind]
        return dev(q, yh, 2 * flip(p, pair) + flip(h, half), z, c)

    def x_peer(d):
        return dev(q, yh, lax.rem(x + d, 4), z, c)

    def q_peer(d):
        return dev(lax.rem(q + d, 4), yh, x, z, c)

    def z_peer(d):
        return dev(q, yh, x, lax.rem(z + d + 12, 12), c)

    def y_peer(d):
        y_ = lax.rem(yh * 4 + q + d, 8)
        return dev(lax.rem(y_, 4), lax.div(y_, 4), x, z, c)

    core_peer = dev(q, yh, x, z, 1 - c)
    started = []

    def remote(src, dst, s, r, to):
        return pltpu.make_async_remote_copy(
            src_ref=src, dst_ref=dst, send_sem=s, recv_sem=r, device_id=to, device_id_type=MESH
        )

    def start(copy):
        copy.start()
        started.append(copy.wait_send)

    barrier = pltpu.get_barrier_semaphore()
    peers = []
    for i in FIRST:
        q_, yh_, h_ = group_peer(i)
        peers.append(dev(q_, yh_, 2 * p + h_, z, c))
    peers += [kind_peer(0), kind_peer(1)] + [z_peer(d) for d in range(1, 12)] + [core_peer]
    for peer in peers:
        pl.semaphore_signal(barrier, inc=1, device_id=peer, device_id_type=MESH)

    loads = [
        pltpu.make_async_copy(
            act.at[:, pl.ds(pl.multiple_of(q * 2048 + flip(h, half) * 1024, 1024), 1024)],
            DA.at[half, pl.ds(128, 128)],
            a_sem.at[half],
        )
        for half in range(2)
    ]
    small_loads = [
        pltpu.make_async_copy(w_any, wv, a_sem.at[2]),
        pltpu.make_async_copy(b_any, bv, a_sem.at[3]),
    ]
    for copy in small_loads + loads:
        copy.start()

    pl.semaphore_wait(barrier, len(peers))

    r_own = q * 4 + yh * 2 + h

    def piece(q_, h_):
        return w_any.at[:, pl.ds(pl.multiple_of((q_ * 2 + h_) * 1024, 1024), 1024)]

    p0 = []
    for i in FIRST:
        q_, yh_, h_ = group_peer(i)
        p0.append(
            remote(
                piece(q_, h_), rbuf.at[r_own], p0_s.at[i], p0_r.at[i],
                dev(q_, yh_, 2 * p + h_, z, c),
            )
        )
    for copy in p0:
        start(copy)
    own = pltpu.make_async_copy(piece(q, h), rbuf.at[r_own], own_sem)
    own.start()

    def place(at):
        near, pair, r = at >> 5, (at >> 4) & 1, at & 15
        far = (near + 1) >> 1
        z_ = z + jnp.where((near & 1) == 1, -far, far)
        z_ = jnp.where(z_ < 0, z_ + 12, jnp.where(z_ >= 12, z_ - 12, z_))
        x_ = 2 * (p + pair - 2 * p * pair) + (r & 1)
        return (r >> 2) * 96 + z_ * 8 + ((r >> 1) & 1) * 4 + x_

    col = lax.broadcasted_iota(jnp.int32, (96, 384), 1)
    row = lax.broadcasted_iota(jnp.int32, (96, 384), 0)
    hot[...] = jnp.where(place(col) == q * 96 + row, 1.0, 0.0).astype(bf16)
    held = place(lax.broadcasted_iota(jnp.int32, (384, 128), 0))
    for i in range(3):
        to = lax.broadcasted_iota(jnp.int32, (384, 128), 1) + i * 128
        turn[:, i * 128 : i * 128 + 128] = jnp.where(held == to, 1.0, 0.0).astype(bf16)
    for copy in small_loads:
        copy.wait()
    bias8 = jnp.broadcast_to(bv[...], (8, 96))
    bias_wide = sum(nn(part, hot[...]) for part in split3(bias8))[0:1, :]
    own.wait()
    for copy in p0:
        copy.wait_recv()
    W[0, 0, 0] = jnp.concatenate([rbuf[i] for i in range(16)], axis=0).astype(bf16)

    def az(t, dz, s):
        to = slot(dz - s) if dz - s != -6 else 11
        return remote(
            W.at[0, slot(dz), t], W.at[0, to, t], az_s.at[t, to], az_r.at[t, to], z_peer(s)
        )

    def wait_z(t, dz):
        b = W.at[0, slot(dz), t]
        remote(b, b, az_s.at[t, slot(dz)], az_r.at[t, slot(dz)], z_peer(1)).wait_recv()

    def ax(kind, dz):
        at = slot(dz)
        half, pair = KINDS[kind]
        return remote(
            W.at[0, at, 0], W.at[half, at, pair], ax_s.at[kind, at], ax_r.at[kind, at],
            kind_peer(kind),
        )

    FAR = (-5, 5, 6)

    def along_x(dz):
        if dz in FAR:
            start(ax(0, dz))
        start(ax(1, dz))
        start(ax(2, dz))

    def wait_x(dz):
        ax(1, dz).wait_recv()
        ax(2, dz).wait_recv()

    STRIDE = (3, 2)

    def onward(t, dz):
        if dz % STRIDE[t]:
            return
        for way in ((1, -1) if dz == 0 else (1,) if dz < 0 else (-1,)):
            for hops in range(STRIDE[t], 0, -1):
                far = abs(dz) + hops
                if far > (6, 4)[t] or (far == 6 and way == -1):
                    continue
                start(az(t, dz, way * hops))

    def pass_on(events):
        for t, dz in events:
            wait_z(t, dz)
            if dz != 6:
                onward(t, dz)
            if t == 0:
                along_x(dz)

    two = remote(W.at[0, 0, 0], W.at[0, 0, 1], ad_s, ad_r, kind_peer(0))
    start(two)
    onward(0, 0)
    along_x(0)
    two.wait_recv()
    onward(1, 0)
    pass_on(((0, -1), (0, 1), (0, -2), (0, 2), (0, -3), (0, 3), (1, -2), (1, 2), (0, -4), (0, 4), (0, -5), (0, 5), (0, 6)))
    for copy in loads:
        copy.wait()

    def rows(half, chunk):
        first, last = CHUNKS[chunk]
        return W[half, first:last].reshape(32 * (last - first), 1024)

    def lanes(chunk):
        first, last = CHUNKS[chunk]
        return slice(32 * first, 32 * last)

    pq, pr, C = (pqa, pqb), (pra, prb), (ca, cb)
    dq, dr, E = (dqa, dqb), (dra, drb), (ea, eb)

    def to_slabs(send, recv, chunk, s, r):
        copies = [
            remote(send.at[lax.rem(q + d, 4)], recv.at[d], s.at[chunk, d], r.at[chunk, d], q_peer(d))
            for d in (2, 1, 3)
        ]
        for copy in copies:
            start(copy)
        return copies

    def share(buffer, chunk, s, r):
        for d in (2, 1, 3):
            start(
                remote(buffer.at[q], buffer.at[q], s.at[chunk, d], r.at[chunk, d], q_peer(d))
            )

    def shared(buffer, chunk, s, r):
        for d in (1, 3, 2):
            b = buffer.at[lax.rem(q + 4 - d, 4)]
            remote(b, b, s.at[chunk, d], r.at[chunk, d], q_peer(d)).wait_recv()
        return buffer[...].reshape(128, buffer.shape[2])

    def make_pre(chunk):
        part = nt(DA[0, 128:256], rows(0, chunk)) + nt(DA[1, 128:256], rows(1, chunk))
        part = part + bias_wide[:, lanes(chunk)]
        pq[chunk][...] = part.reshape(4, 32, part.shape[1])
        return to_slabs(pq[chunk], pr[chunk], chunk, pre_s, pre_r)

    def make_codes(chunk, copies):
        for copy in copies:
            copy.wait_recv()
        s, r = pq[chunk], pr[chunk]
        pre = (s[q] + r[1]) + (r[2] + r[3])
        codes = jnp.maximum(pre, 0.0)
        C[chunk][q] = codes.astype(bf16)
        share(C[chunk], chunk, code_s, code_r)
        return pre, codes

    for dz in (0, -1, 1, -2, 2, -3, 3, -4):
        wait_x(dz)
    for dz in (-1, 1, -3, 3, -4):
        wait_z(1, dz)
    copies_a = make_pre(0)
    wait_z(1, 4)
    for dz in FAR:
        ax(0, dz).wait_recv()
    for dz in (4, -5, 5, 6):
        wait_x(dz)
    copies_b = make_pre(1)
    pre_a, codes_a = make_codes(0, copies_a)

    ones = jnp.ones((8, 1024), bf16)
    for chunk in range(2):
        squares = None
        for half in range(2):
            wide = rows(half, chunk).astype(f32)
            sq = wide * wide
            hi = sq.astype(bf16)
            low = (sq - hi.astype(f32)).astype(bf16)
            part = nt(ones, hi) + nt(ones, low)
            squares = part if squares is None else squares + part
        nrm[q, :, lanes(chunk)] = squares
    for d in (2, 1, 3):
        start(remote(nrm.at[q], nrm.at[q], nm_s.at[d], nm_r.at[d], q_peer(d)))

    pre_b, codes_b = make_codes(1, copies_b)
    low = [shared(C[chunk], chunk, code_s, code_r) for chunk in range(2)]

    core_send = []
    for half in range(2):
        for part_at in range(2):
            cols = slice(part_at * 512, part_at * 512 + 512)
            part = nn(low[0], W[half, 0:8, :, :, cols].reshape(256, 512)) + nn(
                low[1], W[half, 8:12, :, :, cols].reshape(128, 512)
            )
            rown[half, :, cols] = part
            rs[half, :, cols] = part.astype(bf16)
            i = 2 * half + part_at
            lane = pl.ds(part_at * 512, 512)
            copy = remote(
                rs.at[half, :, lane], rr.at[half, :, lane], core_s.at[i], core_r.at[i], core_peer
            )
            start(copy)
            core_send.append(copy)
    for chunk in range(2):
        LT[lanes(chunk), 0:128] = jnp.transpose(low[chunk].astype(f32)).astype(bf16)
    squared = jnp.zeros((1, 128), f32)
    for half in range(2):
        for part_at in range(2):
            cols = slice(part_at * 512, part_at * 512 + 512)
            core_send[2 * half + part_at].wait_recv()
            for t in range(4):
                at = slice(t * 32, t * 32 + 32)
                error = (rown[half, at, cols] + rr[half, at, cols].astype(f32)) - DA[
                    half, 128 + t * 32 : 160 + t * 32, cols
                ].astype(f32)
                DA[half, at, cols] = (error * (2.0 / TOKENS)).astype(bf16)
                squared = squared + fold(jnp.sum(error * error, axis=0, keepdims=True))

    def make_dcode(chunk):
        part = nt(DA[0, 0:128], rows(0, chunk)) + nt(DA[1, 0:128], rows(1, chunk))
        dq[chunk][...] = part.astype(bf16).reshape(4, 32, part.shape[1])
        return to_slabs(dq[chunk], dr[chunk], chunk, dc_s, dc_r)

    def make_dpre(chunk, copies, pre):
        for copy in copies:
            copy.wait_recv()
        s, r = dq[chunk], dr[chunk]
        dcode = (s[q].astype(f32) + r[1].astype(f32)) + (r[2].astype(f32) + r[3].astype(f32))
        norms = norms_all[:, lanes(chunk)]
        dpre = jnp.where(pre > 0, dcode + (sparsity / TOKENS) * norms, 0.0)
        E[chunk][q] = dpre.astype(bf16)
        share(E[chunk], chunk, dp_s, dp_r)
        return dpre, norms

    dcode_b = make_dcode(1)
    dcode_a = make_dcode(0)
    for d in (1, 3, 2):
        b = nrm.at[lax.rem(q + 4 - d, 4)]
        remote(b, b, nm_s.at[d], nm_r.at[d], q_peer(d)).wait_recv()
    norms_all = jnp.sqrt(((nrm[0] + nrm[1]) + (nrm[2] + nrm[3]))[0:1] + 1e-6)
    dpre_b, norms_b = make_dpre(1, dcode_b, pre_b)
    dpre_a, norms_a = make_dpre(0, dcode_a, pre_a)

    def make_grad(chunk):
        first, last = CHUNKS[chunk]
        dpre_low = shared(E[chunk], chunk, dp_s, dp_r)
        LT[lanes(chunk), 128:256] = jnp.transpose(dpre_low.astype(f32)).astype(bf16)
        for half in range(2):
            part = nn(LT[lanes(chunk)], DA[half])
            gs[half, first:last] = part.astype(bf16).reshape(last - first, 2, 16, 1024)

    def gx(at, kind):
        half, pair = KINDS[kind]
        return remote(
            gs.at[half, at, pair], gr.at[kind, at], gx_s.at[kind, at], gx_r.at[kind, at],
            kind_peer(kind),
        )

    make_grad(1)

    @pl.loop(0, 4)
    def _(i):
        for kind in range(3):
            gx(11 - i, kind).start()

    bias_part = jnp.concatenate(
        [jnp.sum(v, axis=0, keepdims=True) for v in (dpre_a, dpre_b)], axis=1
    )
    counts = jnp.concatenate(
        [jnp.sum(v, axis=0, keepdims=True) for v in (codes_a, codes_b)], axis=1
    )
    norms = jnp.concatenate([norms_a, norms_b], axis=1)
    loss_part = 0.5 * squared + sparsity * fold(counts * norms)
    both = jnp.concatenate([bias_part, counts, jnp.zeros((6, 384), f32)], axis=0)
    both = sum(nn(part, turn[...]) for part in split3(both))
    y = yh * 4 + q
    vy[y] = jnp.concatenate(
        [both[0:1, i * 128 : i * 128 + 128] for i in range(3)]
        + [both[1:2, i * 128 : i * 128 + 128] for i in range(3)]
        + [loss_part, jnp.zeros((1, 128), f32)],
        axis=0,
    )
    for d in range(1, 8):
        start(remote(vy.at[y], vy.at[y], vy_s.at[d], vy_r.at[d], y_peer(d)))

    make_grad(0)

    @pl.loop(4, 12)
    def _(i):
        for kind in range(3):
            gx(11 - i, kind).start()

    for done in started:
        done()
    started.clear()

    def x_sent():
        @pl.loop(0, 12)
        def _(i):
            for kind in range(3):
                gx(i, kind).wait_send()

    started.append(x_sent)

    for d in range(1, 8):
        b = vy.at[lax.rem(y + 8 - d, 8)]
        remote(b, b, vy_s.at[d], vy_r.at[d], y_peer(d)).wait_recv()
    v = vy[0]
    for i in range(1, 8):
        v = v + vy[i]
    vz[z] = v
    for d in range(1, 12):
        start(remote(vz.at[z], vz.at[z], vz_s.at[d], vz_r.at[d], z_peer(d)))

    def reduce_x(at):
        for kind in (1, 2, 0):
            gx(at, kind).wait_recv()
        return (gs[0, at, 0].astype(f32) + gr[0, at].astype(f32)) + (
            gr[1, at].astype(f32) + gr[2, at].astype(f32)
        )

    def gz(at):
        far = lax.div(at + 1, 2)
        far = far - jnp.where(far > 3, 3, 0)
        sign = 1 - 2 * lax.rem(at, 2)
        sign = jnp.where(at == 11, 1, sign)
        return remote(hs.at[at], hr.at[at], gz_s.at[at], gz_r.at[at], z_peer(sign * far))

    def send_z(at, more=()):
        part = reduce_x(at)
        for other in more:
            gz(other).wait_recv()
            part = part + hr[other].astype(f32)
        hs[at] = part.astype(bf16)
        gz(at).start()

    @pl.loop(0, 5)
    def _(i):
        send_z(11 - i)

    for d in range(1, 12):
        b = vz.at[lax.rem(z + 12 - d, 12)]
        remote(b, b, vz_s.at[d], vz_r.at[d], z_peer(d)).wait_recv()
    v = vz[0]
    for i in range(1, 12):
        v = v + vz[i]
    vx[x] = v
    for d in range(1, 4):
        start(remote(vx.at[x], vx.at[x], vx_s.at[d], vx_r.at[d], x_peer(d)))

    send_z(6, (8, 10, 11))
    send_z(5, (7, 9))

    @pl.loop(7, 11)
    def _(i):
        send_z(11 - i)

    def z_sent():
        @pl.loop(1, 12)
        def _(k):
            gz(k).wait_send()

    started.append(z_sent)
    hown[...] = reduce_x(0)

    for d in range(1, 4):
        b = vx.at[lax.rem(x + 4 - d, 4)]
        remote(b, b, vx_s.at[d], vx_r.at[d], x_peer(d)).wait_recv()
    v = (vx[0] + vx[1]) + (vx[2] + vx[3])
    vc[0] = v
    vc_send = remote(vc.at[0], vc.at[1], vc_s.at[0], vc_r.at[0], core_peer)
    start(vc_send)

    @pl.loop(0, 6)
    def _(i):
        gz(6 - i).wait_recv()
        hown[...] += hr[6 - i].astype(f32)

    total = hown[...]
    for i in range(16):
        fs[i] = total[i : i + 1]
    mine = (q * 2 + h) * 2 + yh
    fin = []
    for i in FIRST:
        q_, yh_, h_ = group_peer(i)
        fin.append(
            remote(
                fs.at[q_ * 4 + yh_ * 2 + h_], fr.at[mine], fin_s.at[i], fin_r.at[i],
                dev(q_, yh_, 2 * p + h_, z, c),
            )
        )
    for copy in fin:
        start(copy)
    fr[mine] = fs[r_own]

    bias8 = jnp.concatenate([v[0:1], v[1:2], v[2:3]], axis=1)
    bias8 = jnp.broadcast_to(bias8, (8, 384))
    pick = jnp.where(col == q * 96 + row, 1.0, 0.0).astype(bf16)
    bias_grad = sum(nt(part, pick) for part in split3(bias8))[0:1, :]
    lane = lax.broadcasted_iota(jnp.int32, (1, 128), 1)
    own_count = jnp.zeros((1, 128), f32)
    for i in range(3):
        own_count = own_count + jnp.where(lane + i * 128 == q * 96 + g, v[3 + i : 4 + i], 0.0)
    own_count = jnp.sum(own_count, axis=1, keepdims=True)
    vc_send.wait_recv()
    loss = jnp.sum(v[6:7] + vc[1, 6:7], axis=1, keepdims=True) * (1.0 / TOKENS)
    small_ref[...] = jnp.zeros((8, 128), f32)
    small_ref[0:1, 0:96] = bias_grad
    small_ref[1:2, :] = jnp.broadcast_to(loss, (1, 128))

    for done in started[:-15]:
        done()
    own_row = wv[...].astype(bf16).astype(f32)
    own_norm = jnp.sqrt(jnp.sum(own_row * own_row, axis=1, keepdims=True) + 1e-6)
    scale = (sparsity / TOKENS) * own_count / own_norm
    for copy in fin:
        copy.wait_recv()
    for s in range(8):
        at = slice(s * 1024, s * 1024 + 1024)
        grad_ref[:, at] = (fr[2 * s] + fr[2 * s + 1]) + scale * own_row[:, at]

    for done in started[-15:]:
        done()


def step(activations, weight, code_bias):
    dma = pltpu.SemaphoreType.DMA
    vmem = pltpu.VMEM
    return pl.pallas_call(
        kernel,
        out_shape=(
            jax.ShapeDtypeStruct((1, 8192), f32),
            jax.ShapeDtypeStruct((8, 128), f32),
        ),
        in_specs=[pl.BlockSpec(memory_space=pl.ANY)] * 3,
        out_specs=[pl.BlockSpec(memory_space=pltpu.VMEM)] * 2,
        scratch_shapes=[
            vmem((1, 8192), f32),
            vmem((1, 96), f32),
            vmem((16, 1, 1024), f32),
            vmem((2, 12, 2, 16, 1024), bf16),
            vmem((2, 256, 1024), bf16),
            vmem((384, 256), bf16),
            vmem((4, 32, 256), f32), vmem((4, 32, 128), f32),
            vmem((4, 32, 256), f32), vmem((4, 32, 128), f32),
            vmem((4, 32, 256), bf16), vmem((4, 32, 128), bf16),
            vmem((2, 128, 1024), f32),
            vmem((2, 128, 1024), bf16),
            vmem((2, 128, 1024), bf16),
            vmem((4, 32, 256), bf16), vmem((4, 32, 128), bf16),
            vmem((4, 32, 256), bf16), vmem((4, 32, 128), bf16),
            vmem((4, 8, 384), f32),
            vmem((4, 32, 256), bf16), vmem((4, 32, 128), bf16),
            vmem((2, 12, 2, 16, 1024), bf16),
            vmem((3, 12, 16, 1024), bf16),
            vmem((12, 16, 1024), bf16),
            vmem((12, 16, 1024), bf16),
            vmem((16, 1024), f32),
            vmem((16, 1, 1024), f32),
            vmem((16, 1, 1024), f32),
            vmem((4, 8, 128), f32),
            vmem((8, 8, 128), f32),
            vmem((12, 8, 128), f32),
            vmem((2, 8, 128), f32),
            vmem((96, 384), bf16),
            vmem((384, 384), bf16),
            dma((4,)),
            dma,
            dma((16,)), dma((16,)),
            dma((3, 12)), dma((3, 12)),
            dma, dma,
            dma((2, 12)), dma((2, 12)),
            dma((2, 4)), dma((2, 4)),
            dma((2, 4)), dma((2, 4)),
            dma((4,)), dma((4,)),
            dma((2, 4)), dma((2, 4)),
            dma((4,)), dma((4,)),
            dma((2, 4)), dma((2, 4)),
            dma((3, 12)), dma((3, 12)),
            dma((12,)), dma((12,)),
            dma((16,)), dma((16,)),
            dma((4,)), dma((4,)),
            dma((8,)), dma((8,)),
            dma((12,)), dma((12,)),
            dma((1,)), dma((1,)),
        ],
        compiler_params=pltpu.CompilerParams(
            collective_id=0, has_side_effects=True, vmem_limit_bytes=52 * 1024 * 1024
        ),
    )(activations, weight, code_bias.reshape(1, 96))


def per_device(activations, weight, weight_mean, weight_square, code_bias, bias_mean, bias_square):
    grad_own, small = step(activations, weight, code_bias)
    bias_grad = small[0, :96]
    total_loss = small[1, 0]
    after_weight, after_mean, after_square = adam_step(weight, weight_mean, weight_square, grad_own)
    after_bias, after_biasmean, after_biassquare = adam_step(
        code_bias, bias_mean, bias_square, bias_grad
    )
    return (
        after_weight,
        after_mean,
        after_square,
        after_bias,
        after_biasmean,
        after_biassquare,
        total_loss,
    )


def solution(mesh):
    placed = (
        P("dp", None),
        P(("latent", "dp"), None),
        P(("latent", "dp"), None),
        P(("latent", "dp"), None),
        P("latent"),
        P("latent"),
        P("latent"),
    )
    return jax.shard_map(
        per_device,
        mesh=mesh,
        in_specs=placed,
        out_specs=(
            P(("latent", "dp"), None),
            P(("latent", "dp"), None),
            P(("latent", "dp"), None),
            P("latent"),
            P("latent"),
            P("latent"),
            P(),
        ),
        check_vma=False,
    )
```
